256 devices in a mesh: dp: 4 (over x), tm: 64 (over z, y, core).
Axes of the slice: x: 4, y: 4, z: 8, core: 2. Of those that a mesh axis runs over, the one named last changes fastest.
Arguments:
- queries: bfloat16 [512, 64, 1536], P(('dp', 'tm')), parts along dimension 0, may hold values from -6 to 6
- key_states: bfloat16 [512, 64, 1536], P(('dp', 'tm')), parts along dimension 0, may hold values from -6 to 6
- value_states: bfloat16 [512, 64, 1536], P(('dp', 'tm')), parts along dimension 0, may hold values from -6 to 6
- clip_ids: int32 [512], P(('dp', 'tm')), parts along dimension 0, may hold values from 0 to 7, never falling along the last dimension, each value on 1 to 80 neighbouring positions
Outputs:
- attended: bfloat16 [512, 64, 1536], P(('dp', 'tm')), parts along dimension 0
The draws below stay inside these ranges and needn't reach their ends.
There are 4 independent parts, one for each index of `dp`. The reference program is written for one: setup_inputs(seed, part) draws one part's arguments, and reference() takes and returns one part's arrays. A program takes and returns all parts, laid end to end along the dimension named above; each array names one. Nothing has to cross between parts.
All inputs are finite; a program needn't handle non-finite values.
Results may differ from the reference program's by a relative error of at most 0.003.
Values may be sent and summed in bfloat16 or wider, within the bound.
A program may use at most 256 MiB of HBM per device.

```python
import math
import jax
import jax.numpy as jnp
import numpy as np
from jax import lax

HEADS = 24
HEAD_DIM = 64
D = 1536
SIDE = 8
TOK = 64
NEAR = 2
FRAMES = 128
CLIP = 80
CLIPS = 8


def shared_direction(key):
    return jax.random.rademacher(jax.random.fold_in(key, 11), (D,), jnp.float32)


def quarter_offsets(key):
    quarters = SIDE // 4 * (SIDE // 4)
    uniform_draw = jax.random.uniform(key, (FRAMES, quarters), jnp.float32, -1.0, 1.0)
    centred = uniform_draw - jnp.mean(uniform_draw, axis=1, keepdims=True)
    tokens = jnp.arange(TOK)
    quarter_index = tokens // SIDE // 4 * (SIDE // 4) + tokens % SIDE // 4
    one_hot = (quarter_index[:, None] == jnp.arange(quarters)[None, :]).astype(jnp.float32)
    return 0.6 * jnp.sum(centred[:, None, :] * one_hot[None, :, :], axis=2)


def draw_queries(key, part):
    direction = shared_direction(key)
    key = jax.random.fold_in(key, 3)
    strength = jax.random.uniform(jax.random.fold_in(key, 21), (FRAMES, TOK, 1), jnp.float32, 0.35, 0.65)
    drawn = jax.random.normal(key, (FRAMES, TOK, D), jnp.float32)
    return jnp.clip(drawn + strength * direction[None, None, :], -6.0, 6.0).astype(jnp.bfloat16)


def draw_key_states(key, part):
    direction = shared_direction(key)
    key = jax.random.fold_in(key, 7)
    offsets = quarter_offsets(jax.random.fold_in(key, 13))
    lifted = (0.6 + offsets)[:, :, None] * direction[None, None, :]
    drawn = jax.random.normal(key, (FRAMES, TOK, D), jnp.float32)
    return jnp.clip(drawn + lifted, -6.0, 6.0).astype(jnp.bfloat16)


def draw_value_states(key, part):
    key = jax.random.fold_in(key, 5)
    direction = jax.random.rademacher(jax.random.fold_in(key, 1), (D,), jnp.float32)
    phase_shift = jax.random.uniform(jax.random.fold_in(key, 2), (), jnp.float32, 0.0, 2.0 * math.pi)
    frames = jnp.arange(FRAMES, dtype=jnp.float32)
    drift_level = 1.2 * jnp.cos(2.0 * math.pi * frames / FRAMES + phase_shift)
    fresh_values = jax.random.normal(key, (FRAMES, TOK, D), jnp.float32)
    return jnp.clip(fresh_values + drift_level[:, None, None] * direction[None, None, :], -6.0, 6.0).astype(jnp.bfloat16)


def profile(amount, total, bound, slope):
    loads = [(1 << 20) // math.isqrt(grade ** slope) + 1 for grade in range(2, amount + 1)]
    surplus, holding = total - bound - (amount - 1), [1] * (amount - 1)
    while surplus > 0:
        free = [i for i in range(amount - 1) if holding[i] < bound]
        pool, left = sum([loads[i] for i in free]), surplus
        for i in free:
            extra = min(bound - holding[i], max(1, left * loads[i] // pool), surplus)
            holding[i] = holding[i] + extra
            surplus = surplus - extra
    return np.array([bound] + holding)


def uneven_parts(stream_key, count, total, limit, lean):
    if count == 2:
        one = jax.random.randint(stream_key, (), max(1, total - limit), min(limit, total - 1) + 1)
        return jnp.stack([one, total - one])
    lengths = jnp.asarray(profile(count, total, limit, lean), jnp.int32)
    twos = (count - 1) // 2
    giver, taker = lengths[1:1 + 2 * twos:2], lengths[2:2 + 2 * twos:2]
    slack = jnp.minimum(giver - 1, limit - taker)
    shifted = jax.random.randint(jax.random.fold_in(stream_key, 1), (twos,), 0, 1 << 20) % (slack + 1)
    lengths = lengths.at[1:1 + 2 * twos:2].set(giver - shifted).at[2:2 + 2 * twos:2].set(taker + shifted)
    return lengths[jax.random.permutation(jax.random.fold_in(stream_key, 2), count)]


def setup_inputs(seed: int = 0, part: int = 0) -> dict:
    seeds = jax.random.split(jax.random.key(seed), 5)
    part_keys = jax.random.split(jax.random.fold_in(seeds[4], part), 5)
    return {
        "queries": draw_queries(jax.random.fold_in(jax.random.fold_in(seeds[4], part), 71), part),
        "key_states": draw_key_states(jax.random.fold_in(jax.random.fold_in(seeds[4], part), 71), part),
        "value_states": draw_value_states(jax.random.fold_in(jax.random.fold_in(seeds[4], part), 71), part),
        "clip_ids": jnp.searchsorted(jnp.cumsum(uneven_parts(part_keys[3], CLIPS, FRAMES, CLIP, 1)), jnp.arange(FRAMES), side="right").astype(jnp.int32),
    }


def pooled_grid(states, stride):
    frame_count = states.shape[0]
    cells = SIDE // stride
    grid = states.astype(jnp.float32).reshape(frame_count, cells, stride, cells, stride, states.shape[-1])
    return jnp.mean(grid, axis=(2, 4)).reshape(frame_count, cells * cells, states.shape[-1]).astype(jnp.bfloat16)


def reference(queries, key_states, value_states, clip_ids):
    near_rows = (SIDE // 2) ** 2
    far_rows = (SIDE // 4) ** 2
    scale = HEAD_DIM ** -0.5
    near_keys = jnp.pad(pooled_grid(key_states, 2), ((NEAR, 0), (0, 0), (0, 0)))
    near_values = jnp.pad(pooled_grid(value_states, 2), ((NEAR, 0), (0, 0), (0, 0)))
    far_keys = jnp.pad(pooled_grid(key_states, 4), ((CLIP, 0), (0, 0), (0, 0)))
    far_values = jnp.pad(pooled_grid(value_states, 4), ((CLIP, 0), (0, 0), (0, 0)))
    near_clips = jnp.pad(clip_ids, (NEAR, 0), constant_values=-1)
    far_clips = jnp.pad(clip_ids, (CLIP, 0), constant_values=-1)
    distance = CLIP - jnp.arange(CLIP, dtype=jnp.int32)

    def one_frame(target):
        query_rows = lax.dynamic_index_in_dim(queries, target, 0, keepdims=False)
        own_keys = lax.dynamic_index_in_dim(key_states, target, 0, keepdims=False)
        own_values = lax.dynamic_index_in_dim(value_states, target, 0, keepdims=False)
        window_keys = lax.dynamic_slice_in_dim(near_keys, target, NEAR, 0).reshape(NEAR * near_rows, D)
        window_values = lax.dynamic_slice_in_dim(near_values, target, NEAR, 0).reshape(NEAR * near_rows, D)
        history_keys = lax.dynamic_slice_in_dim(far_keys, target, CLIP, 0).reshape(CLIP * far_rows, D)
        history_values = lax.dynamic_slice_in_dim(far_values, target, CLIP, 0).reshape(CLIP * far_rows, D)
        clip_here = lax.dynamic_index_in_dim(clip_ids, target, 0, keepdims=False)
        near_ok = lax.dynamic_slice_in_dim(near_clips, target, NEAR, 0) == clip_here
        far_ok = (lax.dynamic_slice_in_dim(far_clips, target, CLIP, 0) == clip_here) & (distance > NEAR)
        allowed = jnp.concatenate([jnp.ones((TOK,), jnp.bool_), jnp.repeat(near_ok, near_rows), jnp.repeat(far_ok, far_rows)])
        all_keys = jnp.concatenate([own_keys, window_keys, history_keys]).astype(jnp.float32).reshape(-1, HEADS, HEAD_DIM)
        all_values = jnp.concatenate([own_values, window_values, history_values]).astype(jnp.float32).reshape(-1, HEADS, HEAD_DIM)
        query_heads = query_rows.astype(jnp.float32).reshape(TOK, HEADS, HEAD_DIM)
        scores = jnp.einsum("qhe,khe->hqk", query_heads, all_keys) * scale
        scores = jnp.where(allowed[None, None, :], scores, -jnp.inf)
        highest = jnp.max(scores, axis=-1, keepdims=True)
        weights = jnp.exp(scores - highest)
        totals = jnp.sum(weights, axis=-1)
        rounded = lax.optimization_barrier(weights.astype(jnp.bfloat16)).astype(jnp.float32)
        mixed = jnp.einsum("hqk,khe->qhe", rounded, all_values)
        return (mixed / jnp.transpose(totals)[:, :, None]).reshape(TOK, D).astype(jnp.bfloat16)

    return lax.map(one_frame, jnp.arange(FRAMES, dtype=jnp.int32))
```

```python
import functools

import jax
import jax.numpy as jnp
from jax import lax
from jax.experimental import pallas as pl
from jax.experimental.pallas import tpu as pltpu
from jax.sharding import PartitionSpec as P

HEAD_DIM = 64
SIDE = 8
TOK = 64
NZ, NY, NC = 8, 4, 2
FPC = 4
HALF = 768
PAIRS = HALF // 128
ROWS = FPC * TOK
LANES = 2 * ROWS
FAR = 4
BLK = FPC * FAR
LEVELS = 4
MIXED = LEVELS * NY
OWN = MIXED + NY
SLOTS = OWN + 1
NKF = SLOTS * BLK
NEAR_ROWS = 16
NKN = 5 * NEAR_ROWS
FLAT = (LEVELS + 2) * NY * FPC
BASE = FLAT - NY * FPC
NEG = -1e30
MESH = pl.DeviceIdType.MESH


def iota(shape, dim):
    return lax.broadcasted_iota(jnp.int32, shape, dim)


def remote(src, dst, ss, rs, to):
    return pltpu.make_async_remote_copy(
        src_ref=src, dst_ref=dst, send_sem=ss, recv_sem=rs, device_id={"tm": to}, device_id_type=MESH
    )


def nt(a, b):
    return lax.dot_general(a, b, (((1,), (1,)), ((), ())), preferred_element_type=jnp.float32)


def tn(a, b):
    return lax.dot_general(a, b, (((0,), (0,)), ((), ())), preferred_element_type=jnp.float32)


def kernel(
    q_hbm, k_hbm, v_hbm, clip_ref, out_hbm,
    qb, kb, vb, far, near, qm, clips, bias_far, bias_near, acc, tops, sums, ob,
    in_sem, sib_ss, sib_rs, z_ss, z_rs, y_ss, y_rs, near_ss, near_rs, cy_ss, cy_rs, cz_ss, cz_rs, o_ss, o_rs, o_ls,
):
    d = lax.axis_index("tm")
    z, y, c = d // (NY * NC), lax.rem(d // NC, NY), lax.rem(d, NC)
    chip = d // NC

    def dev(zz, yy, cc):
        return zz * (NY * NC) + yy * NC + cc

    sibling = dev(z, y, 1 - c)

    far[...] = jnp.zeros_like(far)
    near[:, : 2 * NEAR_ROWS] = jnp.zeros((2, 2 * NEAR_ROWS, HALF), jnp.bfloat16)
    clips[...] = jnp.zeros_like(clips)

    barrier = pltpu.get_barrier_semaphore()

    def greet(to):
        pl.semaphore_signal(barrier, inc=1, device_id={"tm": to}, device_id_type=MESH)

    for yy in range(1, NY):
        for cc in range(NC):
            greet(dev(z, lax.rem(y + yy, NY), cc))
    greet(sibling)
    for k in range(1, LEVELS + 2):
        @pl.when(z >= k)
        def _():
            greet(dev(z - k, y, c))

    @pl.when((y == 0) & (z > 0))
    def _():
        greet(dev(z - 1, NY - 1, c))

    lo = pl.multiple_of(c * HALF, 128)
    hi = pl.multiple_of((1 - c) * HALF, 128)
    mine = pl.ds(2 * c, 2)
    local = []
    for n, (src, dst) in enumerate(((k_hbm, kb), (v_hbm, vb), (q_hbm, qb))):
        cp = pltpu.make_async_copy(src.at[:, :, pl.ds(lo, HALF)], dst.at[mine], in_sem.at[n])
        cp.start()
        local.append(cp)

    up = jnp.minimum(NZ - 1 - z, LEVELS + 1)
    next_near = jnp.where((y == NY - 1) & (z < NZ - 1), 1, 0)
    pl.semaphore_wait(barrier, (NY - 1) * NC + 1 + up + next_near)

    halves = []
    for n, (src, dst) in enumerate(((k_hbm, kb), (v_hbm, vb), (q_hbm, qb))):
        cp = remote(src.at[:, :, pl.ds(hi, HALF)], dst.at[mine], sib_ss.at[n], sib_rs.at[n], sibling)
        cp.start()
        halves.append(cp)

    def wait_half(n):
        local[n].wait()
        other = (kb, vb, qb)[n].at[pl.ds(2 * (1 - c), 2)]
        remote(other, other, sib_ss.at[n], sib_rs.at[n], sibling).wait_recv()

    row = y * NC + c
    clips[LEVELS + 1, row] = jnp.concatenate(
        [jnp.full((1, 128), clip_ref[n].astype(jnp.float32)) for n in range(2)], axis=0
    )
    level_sends = []
    for n in range(1, NY * NC):
        to = lax.rem(row + n, NY * NC)
        ref = clips.at[LEVELS + 1, row]
        cp = remote(ref, ref, cy_ss.at[n], cy_rs.at[n], z * (NY * NC) + to)
        cp.start()
        level_sends.append(cp)

    r = iota((NEAR_ROWS * FPC + BLK, ROWS), 0)
    t = iota((NEAR_ROWS * FPC + BLK, ROWS), 1)
    frame, token = t // TOK, lax.rem(t, TOK)
    line, place = token // SIDE, lax.rem(token, SIDE)
    near_row = frame * NEAR_ROWS + (line // 2) * 4 + place // 2
    far_row = NEAR_ROWS * FPC + frame * FAR + (line // 4) * 2 + place // 4
    pool = jnp.where(r == near_row, 0.25, jnp.where(r == far_row, 0.0625, 0.0)).astype(jnp.bfloat16)
    for n, full in enumerate((kb, vb)):
        wait_half(n)
        pooled = jnp.dot(pool, full[...].reshape(ROWS, HALF), preferred_element_type=jnp.float32)
        pooled = pooled.astype(jnp.bfloat16)
        near[n, 2 * NEAR_ROWS :] = pooled[: NEAR_ROWS * FPC]
        far[n, OWN] = pooled[NEAR_ROWS * FPC :]

    def slot(k, col):
        return (k - 1) * NY + col

    for k in range(1, LEVELS + 2):
        @pl.when(z + k < NZ)
        def _():
            remote(far.at[:, OWN], far.at[:, slot(k, y)], z_ss.at[k], z_rs.at[k], dev(z + k, y, c)).start()

    def mixed(delta, src):
        return remote(
            far.at[:, src], far.at[:, MIXED + y], y_ss.at[LEVELS + 1, delta], y_rs.at[LEVELS + 1, delta],
            dev(z, lax.rem(y + delta, NY), c),
        )

    for delta in range(1, NY):
        @pl.when(y + delta < NY)
        def _():
            mixed(delta, OWN).start()

    near_out = remote(
        near.at[:, pl.ds(4 * NEAR_ROWS, 2 * NEAR_ROWS)], near.at[:, pl.ds(0, 2 * NEAR_ROWS)],
        near_ss.at[0], near_rs.at[0], jnp.minimum((chip + 1) * NC + c, NZ * NY * NC - 1),
    )

    @pl.when(chip < NZ * NY - 1)
    def _():
        near_out.start()

    for n in range(1, NY * NC):
        ref = clips.at[LEVELS + 1, lax.rem(row + NY * NC - n, NY * NC)]
        remote(ref, ref, cy_ss.at[n], cy_rs.at[n], d).wait_recv()
    for k in range(1, LEVELS + 2):
        @pl.when(z + k < NZ)
        def _():
            remote(
                clips.at[LEVELS + 1], clips.at[LEVELS + 1 - k], cz_ss.at[k], cz_rs.at[k], dev(z + k, y, c)
            ).start()

    wait_half(2)
    even = iota((TOK, 128), 1) < HEAD_DIM
    for p in range(PAIRS):
        for i in range(FPC):
            part = qb[i, :, p * 128 : (p + 1) * 128] * jnp.bfloat16(HEAD_DIM ** -0.5)
            qm[p, i * 128 : i * 128 + TOK] = jnp.where(even, part, jnp.zeros_like(part))
            qm[p, i * 128 + TOK : (i + 1) * 128] = jnp.where(even, jnp.zeros_like(part), part)

    def spread(k, delta):
        ref = far.at[:, slot(k, y)]
        return remote(ref, ref, y_ss.at[k, delta], y_rs.at[k, delta], dev(z, lax.rem(y + delta, NY), c))

    for k in range(1, LEVELS + 1):
        @pl.when(z >= k)
        def _():
            ref = far.at[:, slot(k, y)]
            remote(ref, ref, z_ss.at[k], z_rs.at[k], d).wait_recv()
            for delta in range(1, NY):
                spread(k, delta).start()

    @pl.when(z >= LEVELS + 1)
    def _():
        ref = far.at[:, MIXED + y]
        remote(ref, ref, z_ss.at[LEVELS + 1], z_rs.at[LEVELS + 1], d).wait_recv()
        for delta in range(1, NY):
            @pl.when(y + delta >= NY)
            def _():
                mixed(delta, MIXED + y).start()

    for k in range(1, LEVELS + 2):
        @pl.when(z >= k)
        def _():
            ref = clips.at[LEVELS + 1 - k]
            remote(ref, ref, cz_ss.at[k], cz_rs.at[k], d).wait_recv()
    flat_clips = clips[...].reshape(FLAT, 128)
    own_first = BASE + 4 * y
    lane = iota((1, 128), 1)
    query_clip = []
    for i in range(FPC):
        at = iota((FLAT, 128), 0) == own_first + i
        query_clip.append(jnp.sum(jnp.where(at, flat_clips, 0.0), axis=0, keepdims=True))
    flat_bf = flat_clips.astype(jnp.bfloat16)

    def key_clips(numbers, rows):
        pick = (numbers == iota((rows, FLAT), 1)).astype(jnp.float32).astype(jnp.bfloat16)
        return jnp.dot(pick, flat_bf, preferred_element_type=jnp.float32)

    def far_numbers(shape):
        n = iota(shape, 0)
        at, frame = n // BLK, lax.rem(n, BLK) // FAR
        col = lax.rem(at, NY)
        regular = (LEVELS - at // NY) * (NY * FPC) + col * FPC + frame
        shared = jnp.where(col < y, BASE, 0) + col * FPC + frame
        return jnp.where(at < MIXED, regular, jnp.where(at < OWN, shared, own_first + frame))

    def near_numbers(shape):
        return own_first - 2 + iota(shape, 0) // NEAR_ROWS

    floor = (LEVELS + 1 - z) * (NY * FPC)
    for numbers, rows, bias in ((near_numbers, NKN, bias_near), (far_numbers, NKF, bias_far)):
        clip_of = key_clips(numbers((rows, FLAT)), rows)
        number = numbers((rows, 128))
        for i in range(FPC):
            distance = own_first + i - number
            seen = (distance >= 1) & (distance <= 2) if rows == NKN else distance > 2
            ok = seen & (number >= floor) & (clip_of == query_clip[i])
            bias[:, i * 128 : (i + 1) * 128] = jnp.where(ok, 0.0, NEG)

    @pl.when(chip > 0)
    def _():
        ref = near.at[:, pl.ds(0, 2 * NEAR_ROWS)]
        remote(ref, ref, near_ss.at[0], near_rs.at[0], d).wait_recv()

    first_head = lax.rem(iota((1, LANES), 1), 128) < TOK

    def pick_head(both):
        return jnp.where(first_head, both[:HEAD_DIM], both[HEAD_DIM:])

    def cols(p):
        return pl.ds(pl.multiple_of(p * 128, 128), 128)

    def close(p, carry):
        qp = qm[p]
        own = jnp.concatenate(
            [nt(kb[i, :, cols(p)], qp[i * 128 : (i + 1) * 128]) for i in range(FPC)], axis=1
        )
        by = nt(near[0, :NKN, cols(p)], qp) + bias_near[...]
        top = jnp.maximum(jnp.max(own, axis=0, keepdims=True), jnp.max(by, axis=0, keepdims=True))
        own = jnp.exp(own - top)
        by = jnp.exp(by - top)
        tops[p] = top
        sums[p] = jnp.sum(own, axis=0, keepdims=True) + jnp.sum(by, axis=0, keepdims=True)
        own = own.astype(jnp.bfloat16)
        mixed_own = jnp.concatenate(
            [tn(vb[i, :, cols(p)], own[:, i * 128 : (i + 1) * 128]) for i in range(FPC)], axis=1
        )
        acc[p] = pick_head(mixed_own + tn(near[1, :NKN, cols(p)], by.astype(jnp.bfloat16)))
        return carry

    lax.fori_loop(0, PAIRS, close, 0)

    for k in range(1, LEVELS + 1):
        @pl.when(z >= k)
        def _():
            for delta in range(1, NY):
                ref = far.at[:, slot(k, lax.rem(y + NY - delta, NY))]
                remote(ref, ref, y_ss.at[k, delta], y_rs.at[k, delta], d).wait_recv()
    for delta in range(1, NY):
        @pl.when((y >= delta) | (z >= LEVELS + 1))
        def _():
            ref = far.at[:, MIXED + lax.rem(y + NY - delta, NY)]
            remote(ref, ref, y_ss.at[LEVELS + 1, delta], y_rs.at[LEVELS + 1, delta], d).wait_recv()

    theirs = pl.ds(2 * (1 - c), 2)

    def out_local(p):
        return pltpu.make_async_copy(
            ob.at[p, mine], out_hbm.at[:, :, pl.ds(pl.multiple_of(lo + p * 128, 128), 128)], o_ls.at[p]
        )

    def out_remote(p):
        return remote(
            ob.at[p, theirs], out_hbm.at[:, :, pl.ds(pl.multiple_of(lo + p * 128, 128), 128)],
            o_ss.at[p], o_rs.at[p], sibling,
        )

    def history(p, carry):
        scores = nt(far[0, :, :, cols(p)].reshape(NKF, 128), qm[p]) + bias_far[...]
        old = tops[p]
        top = jnp.maximum(old, jnp.max(scores, axis=0, keepdims=True))
        weights = jnp.exp(scores - top)
        factor = jnp.exp(old - top)
        total = sums[p] * factor + jnp.sum(weights, axis=0, keepdims=True)
        both = tn(far[1, :, :, cols(p)].reshape(NKF, 128), weights.astype(jnp.bfloat16))
        result = (acc[p] * factor + pick_head(both)) / total
        for i in range(FPC):
            turned = result[:, i * 128 : (i + 1) * 128].T
            ob[p, i] = jnp.concatenate([turned[:TOK], turned[TOK:]], axis=1).astype(jnp.bfloat16)
        out_local(p).start()
        out_remote(p).start()
        return carry

    lax.fori_loop(0, PAIRS, history, 0)

    for p in range(PAIRS):
        out_local(p).wait()
        out_remote(p).wait_send()
        ref = out_hbm.at[:, :, pl.ds(pl.multiple_of(hi + p * 128, 128), 128)]
        remote(ref, ref, o_ss.at[p], o_rs.at[p], sibling).wait_recv()
    for n in range(3):
        halves[n].wait_send()
    for cp in level_sends:
        cp.wait_send()
    for k in range(1, LEVELS + 2):
        @pl.when(z + k < NZ)
        def _():
            remote(far.at[:, OWN], far.at[:, slot(k, y)], z_ss.at[k], z_rs.at[k], d).wait_send()
            remote(clips.at[LEVELS + 1], clips.at[LEVELS + 1 - k], cz_ss.at[k], cz_rs.at[k], d).wait_send()

    @pl.when(chip < NZ * NY - 1)
    def _():
        near_out.wait_send()

    for delta in range(1, NY):
        @pl.when((y + delta < NY) | (z >= LEVELS + 1))
        def _():
            mixed(delta, OWN).wait_send()
        for k in range(1, LEVELS + 1):
            @pl.when(z >= k)
            def _():
                spread(k, delta).wait_send()


def on_device(queries, key_states, value_states, clip_ids):
    bf, f32 = jnp.bfloat16, jnp.float32
    dma = pltpu.SemaphoreType.DMA
    anywhere = pl.BlockSpec(memory_space=pl.ANY)
    return pl.pallas_call(
        kernel,
        out_shape=jax.ShapeDtypeStruct(queries.shape, bf),
        in_specs=[anywhere, anywhere, anywhere, pl.BlockSpec(memory_space=pltpu.SMEM)],
        out_specs=anywhere,
        scratch_shapes=[
            pltpu.VMEM((FPC, TOK, HALF), bf),
            pltpu.VMEM((FPC, TOK, HALF), bf),
            pltpu.VMEM((FPC, TOK, HALF), bf),
            pltpu.VMEM((2, SLOTS, BLK, HALF), bf),
            pltpu.VMEM((2, 6 * NEAR_ROWS, HALF), bf),
            pltpu.VMEM((PAIRS, LANES, 128), bf),
            pltpu.VMEM((LEVELS + 2, NY * NC, 2, 128), f32),
            pltpu.VMEM((NKF, LANES), f32),
            pltpu.VMEM((NKN, LANES), f32),
            pltpu.VMEM((PAIRS, HEAD_DIM, LANES), f32),
            pltpu.VMEM((PAIRS, 1, LANES), f32),
            pltpu.VMEM((PAIRS, 1, LANES), f32),
            pltpu.VMEM((PAIRS, FPC, TOK, 128), bf),
            dma((3,)),
            dma((3,)), dma((3,)),
            dma((LEVELS + 2,)), dma((LEVELS + 2,)),
            dma((LEVELS + 2, NY)), dma((LEVELS + 2, NY)),
            dma((1,)), dma((1,)),
            dma((NY * NC,)), dma((NY * NC,)),
            dma((LEVELS + 2,)), dma((LEVELS + 2,)),
            dma((PAIRS,)), dma((PAIRS,)), dma((PAIRS,)),
        ],
        compiler_params=pltpu.CompilerParams(
            collective_id=0, has_side_effects=True, vmem_limit_bytes=40 << 20
        ),
        cost_estimate=pl.CostEstimate(flops=1 << 30, bytes_accessed=4 << 20, transcendentals=1 << 21),
    )(queries, key_states, value_states, clip_ids)


def solution(mesh):
    frames = P(("dp", "tm"), None, None)
    return jax.shard_map(
        on_device,
        mesh=mesh,
        in_specs=(frames, frames, frames, P(("dp", "tm"))),
        out_specs=frames,
        check_vma=False,
    )
```

```python
import functools

import jax
import jax.numpy as jnp
from jax import lax
from jax.experimental import pallas as pl
from jax.experimental.pallas import tpu as pltpu
from jax.sharding import PartitionSpec as P

HEAD_DIM = 64
SIDE = 8
TOK = 64
NZ, NY, NC = 8, 4, 2
FPC = 4
HALF = 768
PAIRS = HALF // 128
ROWS = FPC * TOK
LANES = 2 * ROWS
FAR = 4
BLK = FPC * FAR
LEVELS = 4
OWN = 0
ORDER = (1, 2, 5, 3, 4)
FIRST = {k: 1 + n * NY for n, k in enumerate(ORDER)}
MIXED = FIRST[LEVELS + 1]
SLOTS = 1 + 5 * NY
EARLY = FIRST[3]
NKF = SLOTS * BLK
NEAR_ROWS = 16
NKN = 5 * NEAR_ROWS
FLAT = (LEVELS + 2) * NY * FPC
BASE = FLAT - NY * FPC
NEG = -1e30
MESH = pl.DeviceIdType.MESH


def iota(shape, dim):
    return lax.broadcasted_iota(jnp.int32, shape, dim)


def remote(src, dst, ss, rs, to):
    return pltpu.make_async_remote_copy(
        src_ref=src, dst_ref=dst, send_sem=ss, recv_sem=rs, device_id={"tm": to}, device_id_type=MESH
    )


def nt(a, b):
    return lax.dot_general(a, b, (((1,), (1,)), ((), ())), preferred_element_type=jnp.float32)


def tn(a, b):
    return lax.dot_general(a, b, (((0,), (0,)), ((), ())), preferred_element_type=jnp.float32)


def kernel(
    q_hbm, k_hbm, v_hbm, clip_hbm, out_hbm,
    clip_ref, qb, kb, vb, far, near, qm, level_clips, clips, bias_far, bias_near, acc, tops, sums, ob,
    in_sem, sib_ss, sib_rs, z_ss, z_rs, y_ss, y_rs, near_ss, near_rs, cy_ss, cy_rs, cz_ss, cz_rs, o_ss, o_rs, o_ls,
):
    d = lax.axis_index("tm")
    z, y, c = d // (NY * NC), lax.rem(d // NC, NY), lax.rem(d, NC)
    chip = d // NC

    def dev(zz, yy, cc):
        return zz * (NY * NC) + yy * NC + cc

    sibling = dev(z, y, 1 - c)

    far[...] = jnp.zeros_like(far)
    near[:, : 2 * NEAR_ROWS] = jnp.zeros((2, 2 * NEAR_ROWS, HALF), jnp.bfloat16)
    clips[...] = jnp.zeros_like(clips)

    barrier = pltpu.get_barrier_semaphore()

    def greet(to):
        pl.semaphore_signal(barrier, inc=1, device_id={"tm": to}, device_id_type=MESH)

    for yy in range(1, NY):
        for cc in range(NC):
            greet(dev(z, lax.rem(y + yy, NY), cc))
    greet(sibling)
    for k in range(1, LEVELS + 2):
        @pl.when(z >= k)
        def _():
            greet(dev(z - k, y, c))

    @pl.when((y == 0) & (z > 0))
    def _():
        greet(dev(z - 1, NY - 1, c))

    lo = pl.multiple_of(c * HALF, 128)
    hi = pl.multiple_of((1 - c) * HALF, 128)
    mine = pl.ds(2 * c, 2)
    local = []
    for n, (src, dst) in enumerate(((k_hbm, kb), (v_hbm, vb), (q_hbm, qb))):
        cp = pltpu.make_async_copy(src.at[:, :, pl.ds(lo, HALF)], dst.at[mine], in_sem.at[n])
        cp.start()
        local.append(cp)

    clip_copy = pltpu.make_async_copy(clip_hbm, clip_ref, in_sem.at[3])
    clip_copy.start()

    up = jnp.minimum(NZ - 1 - z, LEVELS + 1)
    next_near = jnp.where((y == NY - 1) & (z < NZ - 1), 1, 0)
    pl.semaphore_wait(barrier, (NY - 1) * NC + 1 + up + next_near)

    halves = []
    for n, (src, dst) in enumerate(((k_hbm, kb), (v_hbm, vb), (q_hbm, qb))):
        cp = remote(src.at[:, :, pl.ds(hi, HALF)], dst.at[mine], sib_ss.at[n], sib_rs.at[n], sibling)
        cp.start()
        halves.append(cp)

    def wait_half(n):
        local[n].wait()
        other = (kb, vb, qb)[n].at[pl.ds(2 * (1 - c), 2)]
        remote(other, other, sib_ss.at[n], sib_rs.at[n], sibling).wait_recv()

    clip_copy.wait()
    row = y * NC + c
    lane = iota((1, 128), 1)
    level_clips[row] = sum(
        jnp.where(lane == 2 * row + n, clip_ref[n].astype(jnp.float32), 0.0) for n in range(2)
    )
    level_sends = []
    for n in range(1, NY * NC):
        to = lax.rem(row + n, NY * NC)
        ref = level_clips.at[row]
        cp = remote(ref, ref, cy_ss.at[n], cy_rs.at[n], z * (NY * NC) + to)
        cp.start()
        level_sends.append(cp)

    r = iota((NEAR_ROWS * FPC + BLK, ROWS), 0)
    t = iota((NEAR_ROWS * FPC + BLK, ROWS), 1)
    frame, token = t // TOK, lax.rem(t, TOK)
    line, place = token // SIDE, lax.rem(token, SIDE)
    near_row = frame * NEAR_ROWS + (line // 2) * 4 + place // 2
    far_row = NEAR_ROWS * FPC + frame * FAR + (line // 4) * 2 + place // 4
    pool = jnp.where(r == near_row, 0.25, jnp.where(r == far_row, 0.0625, 0.0)).astype(jnp.bfloat16)
    for n, full in enumerate((kb, vb)):
        wait_half(n)
        pooled = jnp.dot(pool, full[...].reshape(ROWS, HALF), preferred_element_type=jnp.float32)
        pooled = pooled.astype(jnp.bfloat16)
        near[n, 2 * NEAR_ROWS :] = pooled[: NEAR_ROWS * FPC]
        far[n, OWN] = pooled[NEAR_ROWS * FPC :]

    def slot(k, col):
        return FIRST[k] + col

    def rise(k):
        return remote(far.at[:, OWN], far.at[:, slot(k, y)], z_ss.at[k], z_rs.at[k], dev(z + k, y, c))

    def start_rise(k):
        @pl.when(z + k < NZ)
        def _():
            rise(k).start()

    def sent_rise(k):
        @pl.when(z + k < NZ)
        def _():
            rise(k).wait_send()

    for k in (1, 2, 5):
        start_rise(k)

    @pl.when(z == NZ - 1 - LEVELS)
    def _():
        rise(4).start()

    def mixed(delta, src):
        return remote(
            far.at[:, src], far.at[:, MIXED + y], y_ss.at[LEVELS + 1, delta], y_rs.at[LEVELS + 1, delta],
            dev(z, lax.rem(y + delta, NY), c),
        )

    for delta in (1, 3, 2):
        @pl.when(y + delta < NY)
        def _():
            mixed(delta, OWN).start()

    near_out = remote(
        near.at[:, pl.ds(4 * NEAR_ROWS, 2 * NEAR_ROWS)], near.at[:, pl.ds(0, 2 * NEAR_ROWS)],
        near_ss.at[0], near_rs.at[0], jnp.minimum((chip + 1) * NC + c, NZ * NY * NC - 1),
    )

    @pl.when(chip < NZ * NY - 1)
    def _():
        near_out.start()

    for n in range(1, NY * NC):
        ref = level_clips.at[lax.rem(row + NY * NC - n, NY * NC)]
        remote(ref, ref, cy_ss.at[n], cy_rs.at[n], d).wait_recv()
    clips[LEVELS + 1] = jnp.sum(level_clips[...], axis=0)
    for k in range(1, LEVELS + 2):
        @pl.when(z + k < NZ)
        def _():
            remote(
                clips.at[LEVELS + 1], clips.at[LEVELS + 1 - k], cz_ss.at[k], cz_rs.at[k], dev(z + k, y, c)
            ).start()

    wait_half(2)
    even = iota((TOK, 128), 1) < HEAD_DIM
    for p in range(PAIRS):
        for i in range(FPC):
            part = qb[i, :, p * 128 : (p + 1) * 128] * jnp.bfloat16(HEAD_DIM ** -0.5)
            qm[p, i * 128 : i * 128 + TOK] = jnp.where(even, part, jnp.zeros_like(part))
            qm[p, i * 128 + TOK : (i + 1) * 128] = jnp.where(even, jnp.zeros_like(part), part)

    def spread(k, delta):
        ref = far.at[:, slot(k, y)]
        return remote(ref, ref, y_ss.at[k, delta], y_rs.at[k, delta], dev(z, lax.rem(y + delta, NY), c))

    def arrived(k):
        ref = far.at[:, slot(k, y)]
        remote(ref, ref, z_ss.at[k], z_rs.at[k], d).wait_recv()

    def forward():
        return remote(far.at[:, slot(2, y)], far.at[:, slot(3, y)], z_ss.at[3], z_rs.at[3], dev(z + 1, y, c))

    def backward():
        return remote(far.at[:, slot(5, y)], far.at[:, slot(4, y)], z_ss.at[4], z_rs.at[4], dev(z - 1, y, c))

    def pass_on(k):
        @pl.when(z >= k)
        def _():
            arrived(k)
            if k == 2:
                @pl.when(z < NZ - 1)
                def _():
                    forward().start()
            if k == 5:
                backward().start()
            for delta in (1, 3, 2):
                if k <= LEVELS:
                    spread(k, delta).start()
                else:
                    @pl.when(y + delta >= NY)
                    def _():
                        mixed(delta, MIXED + y).start()

    pass_on(1)
    pass_on(2)
    pass_on(5)

    for k in range(1, LEVELS + 2):
        @pl.when(z >= k)
        def _():
            ref = clips.at[LEVELS + 1 - k]
            remote(ref, ref, cz_ss.at[k], cz_rs.at[k], d).wait_recv()
    table = clips[...].reshape(8, 128)
    own_first = BASE + 4 * y
    query_clip = [
        jnp.sum(jnp.where(lane == 4 * y + i, table[LEVELS + 1 : LEVELS + 2], 0.0), axis=1, keepdims=True)
        for i in range(FPC)
    ]
    table = table.astype(jnp.bfloat16)
    ones = jnp.ones((128, 128), jnp.bfloat16)

    def key_clips(numbers, rows):
        pick = (numbers // (NY * FPC))[:, :8] == iota((rows, 8), 1)
        level = jnp.dot(pick.astype(jnp.float32).astype(jnp.bfloat16), table, preferred_element_type=jnp.float32)
        one = jnp.where(lax.rem(numbers, NY * FPC) == iota((rows, 128), 1), level, 0.0)
        return jnp.dot(one.astype(jnp.bfloat16), ones, preferred_element_type=jnp.float32)

    def far_numbers(shape):
        n = iota(shape, 0)
        at, frame = n // BLK, lax.rem(n, BLK) // FAR
        step = at + NY - 1
        col = lax.rem(step, NY)
        level = functools.reduce(
            lambda found, k: jnp.where(step // NY == ORDER.index(k) + 1, k, found), ORDER, 0
        )
        regular = (LEVELS + 1 - level) * (NY * FPC) + col * FPC + frame
        shared = jnp.where(col < y, BASE, 0) + col * FPC + frame
        held = jnp.where((at >= MIXED) & (at < MIXED + NY), shared, regular)
        return jnp.where(at == OWN, own_first + frame, held)

    def near_numbers(shape):
        return own_first - 2 + iota(shape, 0) // NEAR_ROWS

    floor = (LEVELS + 1 - z) * (NY * FPC)
    for numbers, rows, bias in ((near_numbers, NKN, bias_near), (far_numbers, NKF, bias_far)):
        number = numbers((rows, 128))
        clip_of = key_clips(number, rows)
        for i in range(FPC):
            distance = own_first + i - number
            seen = (distance >= 1) & (distance <= 2) if rows == NKN else distance > 2
            ok = seen & (number >= floor) & (clip_of == query_clip[i])
            bias[:, i * 128 : (i + 1) * 128] = jnp.where(ok, 0.0, NEG)

    @pl.when(chip > 0)
    def _():
        ref = near.at[:, pl.ds(0, 2 * NEAR_ROWS)]
        remote(ref, ref, near_ss.at[0], near_rs.at[0], d).wait_recv()

    first_head = lax.rem(iota((1, LANES), 1), 128) < TOK

    def pick_head(both):
        return jnp.where(first_head, both[:HEAD_DIM], both[HEAD_DIM:])

    def cols(p):
        return pl.ds(pl.multiple_of(p * 128, 128), 128)

    def close(p, carry):
        qp = qm[p]
        own = jnp.concatenate(
            [nt(kb[i, :, cols(p)], qp[i * 128 : (i + 1) * 128]) for i in range(FPC)], axis=1
        )
        by = nt(near[0, :NKN, cols(p)], qp) + bias_near[...]
        top = jnp.maximum(jnp.max(own, axis=0, keepdims=True), jnp.max(by, axis=0, keepdims=True))
        own = jnp.exp(own - top)
        by = jnp.exp(by - top)
        tops[p] = top
        sums[p] = jnp.sum(own, axis=0, keepdims=True) + jnp.sum(by, axis=0, keepdims=True)
        own = own.astype(jnp.bfloat16)
        mixed_own = jnp.concatenate(
            [tn(vb[i, :, cols(p)], own[:, i * 128 : (i + 1) * 128]) for i in range(FPC)], axis=1
        )
        acc[p] = pick_head(mixed_own + tn(near[1, :NKN, cols(p)], by.astype(jnp.bfloat16)))
        return carry

    lax.fori_loop(0, 4, close, 0)
    pass_on(3)
    pass_on(4)
    lax.fori_loop(4, PAIRS, close, 0)

    def level_here(k):
        @pl.when(z >= k)
        def _():
            for delta in range(1, NY):
                ref = far.at[:, slot(k, lax.rem(y + NY - delta, NY))]
                remote(ref, ref, y_ss.at[k, delta], y_rs.at[k, delta], d).wait_recv()

    level_here(1)
    level_here(2)
    for delta in range(1, NY):
        @pl.when((y >= delta) | (z >= LEVELS + 1))
        def _():
            ref = far.at[:, MIXED + lax.rem(y + NY - delta, NY)]
            remote(ref, ref, y_ss.at[LEVELS + 1, delta], y_rs.at[LEVELS + 1, delta], d).wait_recv()

    theirs = pl.ds(2 * (1 - c), 2)

    def out_local(p):
        return pltpu.make_async_copy(
            ob.at[p, mine], out_hbm.at[:, :, pl.ds(pl.multiple_of(lo + p * 128, 128), 128)], o_ls.at[p]
        )

    def out_remote(p):
        return remote(
            ob.at[p, theirs], out_hbm.at[:, :, pl.ds(pl.multiple_of(lo + p * 128, 128), 128)],
            o_ss.at[p], o_rs.at[p], sibling,
        )

    def history(p, first, last):
        rows = (last - first) * BLK
        keys = far[0, first:last, :, cols(p)].reshape(rows, 128)
        scores = nt(keys, qm[p]) + bias_far[first * BLK : last * BLK]
        old = tops[p]
        top = jnp.maximum(old, jnp.max(scores, axis=0, keepdims=True))
        weights = jnp.exp(scores - top)
        factor = jnp.exp(old - top)
        total = sums[p] * factor + jnp.sum(weights, axis=0, keepdims=True)
        both = tn(far[1, first:last, :, cols(p)].reshape(rows, 128), weights.astype(jnp.bfloat16))
        return top, total, acc[p] * factor + pick_head(both)

    def early(p, carry):
        tops[p], sums[p], acc[p] = history(p, 0, EARLY)
        return carry

    def late(p, carry):
        _, total, summed = history(p, EARLY, SLOTS)
        result = summed / total
        for i in range(FPC):
            turned = result[:, i * 128 : (i + 1) * 128].T
            ob[p, i] = jnp.concatenate([turned[:TOK], turned[TOK:]], axis=1).astype(jnp.bfloat16)
        out_local(p).start()
        out_remote(p).start()
        return carry

    lax.fori_loop(0, PAIRS, early, 0)
    level_here(3)
    level_here(4)
    lax.fori_loop(0, PAIRS, late, 0, unroll=True)

    for p in range(PAIRS):
        out_local(p).wait()
        out_remote(p).wait_send()
        ref = out_hbm.at[:, :, pl.ds(pl.multiple_of(hi + p * 128, 128), 128)]
        remote(ref, ref, o_ss.at[p], o_rs.at[p], sibling).wait_recv()
    for n in range(3):
        halves[n].wait_send()
    for cp in level_sends:
        cp.wait_send()
    for k in (1, 2, 5):
        sent_rise(k)

    @pl.when(z == NZ - 1 - LEVELS)
    def _():
        rise(4).wait_send()

    @pl.when(z >= 5)
    def _():
        backward().wait_send()


    @pl.when((z >= 2) & (z < NZ - 1))
    def _():
        forward().wait_send()

    for k in range(1, LEVELS + 2):
        @pl.when(z + k < NZ)
        def _():
            remote(clips.at[LEVELS + 1], clips.at[LEVELS + 1 - k], cz_ss.at[k], cz_rs.at[k], d).wait_send()

    @pl.when(chip < NZ * NY - 1)
    def _():
        near_out.wait_send()

    for delta in range(1, NY):
        @pl.when((y + delta < NY) | (z >= LEVELS + 1))
        def _():
            mixed(delta, OWN).wait_send()
        for k in range(1, LEVELS + 1):
            @pl.when(z >= k)
            def _():
                spread(k, delta).wait_send()


def on_device(queries, key_states, value_states, clip_ids):
    bf, f32 = jnp.bfloat16, jnp.float32
    dma = pltpu.SemaphoreType.DMA
    anywhere = pl.BlockSpec(memory_space=pltpu.HBM)
    return pl.pallas_call(
        kernel,
        out_shape=jax.ShapeDtypeStruct(queries.shape, bf),
        in_specs=[anywhere] * 4,
        out_specs=anywhere,
        scratch_shapes=[
            pltpu.SMEM((2,), jnp.int32),
            pltpu.VMEM((FPC, TOK, HALF), bf),
            pltpu.VMEM((FPC, TOK, HALF), bf),
            pltpu.VMEM((FPC, TOK, HALF), bf),
            pltpu.VMEM((2, SLOTS, BLK, HALF), bf),
            pltpu.VMEM((2, 6 * NEAR_ROWS, HALF), bf),
            pltpu.VMEM((PAIRS, LANES, 128), bf),
            pltpu.VMEM((NY * NC, 1, 128), f32),
            pltpu.VMEM((8, 1, 128), f32),
            pltpu.VMEM((NKF, LANES), f32),
            pltpu.VMEM((NKN, LANES), f32),
            pltpu.VMEM((PAIRS, HEAD_DIM, LANES), f32),
            pltpu.VMEM((PAIRS, 1, LANES), f32),
            pltpu.VMEM((PAIRS, 1, LANES), f32),
            pltpu.VMEM((PAIRS, FPC, TOK, 128), bf),
            dma((4,)),
            dma((3,)), dma((3,)),
            dma((LEVELS + 2,)), dma((LEVELS + 2,)),
            dma((LEVELS + 2, NY)), dma((LEVELS + 2, NY)),
            dma((1,)), dma((1,)),
            dma((NY * NC,)), dma((NY * NC,)),
            dma((LEVELS + 2,)), dma((LEVELS + 2,)),
            dma((PAIRS,)), dma((PAIRS,)), dma((PAIRS,)),
        ],
        compiler_params=pltpu.CompilerParams(
            collective_id=0, has_side_effects=True, vmem_limit_bytes=64 << 20
        ),
        cost_estimate=pl.CostEstimate(flops=1 << 30, bytes_accessed=4 << 20, transcendentals=1 << 21),
    )(queries, key_states, value_states, clip_ids)


def solution(mesh):
    frames = P(("dp", "tm"), None, None)
    return jax.shard_map(
        on_device,
        mesh=mesh,
        in_specs=(frames, frames, frames, P(("dp", "tm"))),
        out_specs=frames,
        check_vma=False,
    )
```

```python
import functools

import jax
import jax.numpy as jnp
from jax import lax
from jax.experimental import pallas as pl
from jax.experimental.pallas import tpu as pltpu
from jax.sharding import PartitionSpec as P

HEAD_DIM = 64
SIDE = 8
TOK = 64
NZ, NY, NC = 8, 4, 2
FPC = 4
HALF = 768
PAIRS = HALF // 128
ROWS = FPC * TOK
LANES = 2 * ROWS
FAR = 4
BLK = FPC * FAR
LEVELS = 4
OWN = 0
ORDER = (1, 2, 5, 3, 4)
FIRST = {k: 1 + n * NY for n, k in enumerate(ORDER)}
DIRECT = (1, 2, 5)
CHAINED = (2, 3)
MIXED = FIRST[LEVELS + 1]
SLOTS = 1 + 5 * NY
EARLY = FIRST[3]
NKF = SLOTS * BLK
NEAR_ROWS = 16
NKN = 5 * NEAR_ROWS
FLAT = (LEVELS + 2) * NY * FPC
BASE = FLAT - NY * FPC
NEG = -1e30
MESH = pl.DeviceIdType.MESH


def iota(shape, dim):
    return lax.broadcasted_iota(jnp.int32, shape, dim)


def remote(src, dst, ss, rs, to):
    return pltpu.make_async_remote_copy(
        src_ref=src, dst_ref=dst, send_sem=ss, recv_sem=rs, device_id={"tm": to}, device_id_type=MESH
    )


def nt(a, b):
    return lax.dot_general(a, b, (((1,), (1,)), ((), ())), preferred_element_type=jnp.float32)


def nn(a, b):
    return jnp.dot(a, b, preferred_element_type=jnp.float32)


def tn(a, b):
    return lax.dot_general(a, b, (((0,), (0,)), ((), ())), preferred_element_type=jnp.float32)


def kernel(
    q_hbm, k_hbm, v_hbm, clip_hbm, out_hbm,
    clip_ref, kf, vf, qb, kb, vb, pooled, far, near, qm, level_clips, clips, bias_far, bias_near, acc, tops, sums, ob,
    in_sem, sib_ss, sib_rs, own_ss, own_rs, z_ss, z_rs, m_ss, m_rs, y_ss, y_rs, x_ss,
    near_ss, near_rs, cy_ss, cy_rs, cz_ss, cz_rs, o_ss, o_rs, o_ls,
):
    d = lax.axis_index("tm")
    z, y, c = d // (NY * NC), lax.rem(d // NC, NY), lax.rem(d, NC)
    chip = d // NC

    def dev(zz, yy, cc):
        return zz * (NY * NC) + yy * NC + cc

    sibling = dev(z, y, 1 - c)

    lo = pl.multiple_of(c * HALF, 128)
    hi = pl.multiple_of((1 - c) * HALF, 128)
    mine = pl.ds(2 * c, 2)
    whole = []
    for n, (src, dst) in enumerate(((k_hbm, kf), (v_hbm, vf))):
        cp = pltpu.make_async_copy(src, dst, in_sem.at[n])
        cp.start()
        whole.append(cp)
    clip_copy = pltpu.make_async_copy(clip_hbm, clip_ref, in_sem.at[2])
    clip_copy.start()
    local = []
    for n, (src, dst) in enumerate(((k_hbm, kb), (v_hbm, vb), (q_hbm, qb))):
        cp = pltpu.make_async_copy(src.at[:, :, pl.ds(lo, HALF)], dst.at[mine], in_sem.at[3 + n])
        cp.start()
        local.append(cp)

    far[...] = jnp.zeros_like(far)
    near[:, : 2 * NEAR_ROWS] = jnp.zeros((2, 2 * NEAR_ROWS, HALF), jnp.bfloat16)
    clips[...] = jnp.zeros_like(clips)

    barrier = pltpu.get_barrier_semaphore()

    def greet(to):
        pl.semaphore_signal(barrier, inc=1, device_id={"tm": to}, device_id_type=MESH)

    for yy in range(1, NY):
        for cc in range(NC):
            greet(dev(z, lax.rem(y + yy, NY), cc))
    greet(sibling)
    for k in range(1, LEVELS + 2):
        @pl.when(z >= k)
        def _():
            greet(dev(z - k, y, c))
            if k in DIRECT:
                greet(dev(z - k, y, 1 - c))

    last_rise = NZ - 1 - LEVELS

    @pl.when(z == NZ - 1)
    def _():
        greet(dev(last_rise, y, 1 - c))

    @pl.when((y == 0) & (z > 0))
    def _():
        greet(dev(z - 1, NY - 1, c))

    def pool_matrix(rows, frames, side):
        r, t = iota((rows, frames * TOK), 0), iota((rows, frames * TOK), 1)
        frame, token = t // TOK, lax.rem(t, TOK)
        cells = SIDE // side
        at = frame * cells * cells + (token // SIDE // side) * cells + lax.rem(token, SIDE) // side
        return jnp.where(r == at, 1.0 / (side * side), 0.0).astype(jnp.bfloat16)

    far_pool = pool_matrix(2 * FAR, 2, 4)
    means = []
    for n, full in enumerate((kf, vf)):
        whole[n].wait()
        means.append(nn(far_pool, full[...].reshape(2 * TOK, 2 * HALF)))
    means = jnp.concatenate(means, axis=0).astype(jnp.bfloat16)
    for n in range(2):
        pooled[n] = means[:, n * HALF : (n + 1) * HALF]

    up = jnp.minimum(NZ - 1 - z, LEVELS + 1)
    crossing = sum(jnp.where(z + k < NZ, 1, 0) for k in DIRECT) + jnp.where(z == last_rise, 1, 0)
    next_near = jnp.where((y == NY - 1) & (z < NZ - 1), 1, 0)
    pl.semaphore_wait(barrier, (NY - 1) * NC + 1 + up + crossing + next_near)

    def slot(k, col):
        return FIRST[k] + col

    def rise(k, core):
        return remote(
            pooled.at[core], far.at[slot(k, y), c], z_ss.at[k, core], z_rs.at[k, c], dev(z + k, y, core)
        )

    def mixed(delta, core):
        return remote(
            pooled.at[core], far.at[MIXED + y, c], m_ss.at[delta, core], m_rs.at[delta, c],
            dev(z, lax.rem(y + delta, NY), core),
        )

    def each_rise(act):
        for k in DIRECT:
            @pl.when(z + k < NZ)
            def _():
                for core in range(NC):
                    act(rise(k, core))

        @pl.when(z == last_rise)
        def _():
            for core in range(NC):
                act(rise(LEVELS, core))

    def each_mixed(act):
        for delta in (1, 3, 2):
            @pl.when(y + delta < NY)
            def _():
                for core in range(NC):
                    act(mixed(delta, core))

    each_rise(lambda cp: cp.start())
    each_mixed(lambda cp: cp.start())
    across = remote(pooled.at[1 - c], far.at[OWN, c], own_ss.at[0], own_rs.at[0], sibling)
    across.start()
    far[OWN, c] = pooled[c]

    halves = []
    for n, (src, dst) in enumerate(((k_hbm, kb), (v_hbm, vb), (q_hbm, qb))):
        cp = remote(src.at[:, :, pl.ds(hi, HALF)], dst.at[mine], sib_ss.at[n], sib_rs.at[n], sibling)
        cp.start()
        halves.append(cp)

    def wait_half(n):
        local[n].wait()
        other = (kb, vb, qb)[n].at[pl.ds(2 * (1 - c), 2)]
        remote(other, other, sib_ss.at[n], sib_rs.at[n], sibling).wait_recv()

    clip_copy.wait()
    row = y * NC + c
    lane = iota((1, 128), 1)
    level_clips[row] = sum(
        jnp.where(lane == 2 * row + n, clip_ref[n].astype(jnp.float32), 0.0) for n in range(2)
    )
    level_sends = []
    for n in range(1, NY * NC):
        to = lax.rem(row + n, NY * NC)
        ref = level_clips.at[row]
        cp = remote(ref, ref, cy_ss.at[n], cy_rs.at[n], z * (NY * NC) + to)
        cp.start()
        level_sends.append(cp)

    near_pool = pool_matrix(NEAR_ROWS * FPC, FPC, 2)
    for n, full in enumerate((kb, vb)):
        wait_half(n)
        near[n, 2 * NEAR_ROWS :] = nn(near_pool, full[...].reshape(ROWS, HALF)).astype(jnp.bfloat16)

    near_out = remote(
        near.at[:, pl.ds(4 * NEAR_ROWS, 2 * NEAR_ROWS)], near.at[:, pl.ds(0, 2 * NEAR_ROWS)],
        near_ss.at[0], near_rs.at[0], jnp.minimum((chip + 1) * NC + c, NZ * NY * NC - 1),
    )

    @pl.when(chip < NZ * NY - 1)
    def _():
        near_out.start()

    for n in range(1, NY * NC):
        ref = level_clips.at[lax.rem(row + NY * NC - n, NY * NC)]
        remote(ref, ref, cy_ss.at[n], cy_rs.at[n], d).wait_recv()
    clips[LEVELS + 1] = jnp.sum(level_clips[...], axis=0)
    for k in range(1, LEVELS + 2):
        @pl.when(z + k < NZ)
        def _():
            remote(
                clips.at[LEVELS + 1], clips.at[LEVELS + 1 - k], cz_ss.at[k], cz_rs.at[k], dev(z + k, y, c)
            ).start()

    def spread(k, delta):
        ref = far.at[slot(k, y)]
        return remote(ref, ref, y_ss.at[k, delta], y_rs.at[k, delta], dev(z, lax.rem(y + delta, NY), c))

    def arrived(k, part):
        ref = far.at[slot(k, y), part]
        remote(ref, ref, z_ss.at[k, 0], z_rs.at[k, part], d).wait_recv()

    def arrived_whole(k):
        ref = far.at[slot(k, y)]
        remote(ref, ref, z_ss.at[k, 0], z_rs.at[k, 0], d).wait_recv()

    def forward():
        return remote(far.at[slot(2, y)], far.at[slot(3, y)], z_ss.at[3, 0], z_rs.at[3, 0], dev(z + 1, y, c))

    def backward():
        return remote(far.at[slot(5, y)], far.at[slot(4, y)], z_ss.at[4, 0], z_rs.at[4, 0], dev(z - 1, y, c))

    def spread_to(k):
        return (1, 3) if k in CHAINED else (1, 3, 2)

    def pass_on(k):
        @pl.when(z >= k)
        def _():
            if k in DIRECT:
                for part in range(NC):
                    arrived(k, part)
            elif k == LEVELS:
                @pl.when(z == NZ - 1)
                def _():
                    for part in range(NC):
                        arrived(k, part)

                @pl.when(z < NZ - 1)
                def _():
                    arrived_whole(k)
            else:
                arrived_whole(k)
            if k == 2:
                @pl.when(z < NZ - 1)
                def _():
                    forward().start()
            if k == LEVELS + 1:
                backward().start()
            for delta in spread_to(k):
                if k <= LEVELS:
                    spread(k, delta).start()
                else:
                    @pl.when(y + delta >= NY)
                    def _():
                        spread(k, delta).start()

    opposite = lax.rem(y + 2, NY)

    def chain(k):
        return remote(
            far.at[slot(k - 1, opposite)], far.at[slot(k, opposite)], x_ss.at[k], y_rs.at[k, 2], dev(z + 1, y, c)
        )

    def came(k, delta):
        ref = far.at[slot(k, lax.rem(y + NY - delta, NY))]
        remote(ref, ref, y_ss.at[k, delta], y_rs.at[k, delta], d).wait_recv()

    def chain_on(k):
        if k not in CHAINED:
            return

        @pl.when(z >= k - 1)
        def _():
            came(k - 1, 2)

            @pl.when(z < NZ - 1)
            def _():
                chain(k).start()

    pass_on(1)

    wait_half(2)
    even = iota((TOK, 128), 1) < HEAD_DIM
    for p in range(PAIRS):
        for i in range(FPC):
            part = qb[i, :, p * 128 : (p + 1) * 128] * jnp.bfloat16(HEAD_DIM ** -0.5)
            apart = jnp.concatenate(
                [jnp.where(even, part, jnp.zeros_like(part)), jnp.where(even, jnp.zeros_like(part), part)], axis=0
            )
            qm[p, :, i * 128 : (i + 1) * 128] = apart.T

    first_head = lax.rem(iota((1, LANES), 1), 128) < TOK

    def pick_head(both):
        return jnp.where(first_head, both[:HEAD_DIM], both[HEAD_DIM:])

    def cols(p):
        return pl.ds(pl.multiple_of(p * 128, 128), 128)

    def own_frame(p, carry):
        qp = qm[p]
        scores = jnp.concatenate(
            [nn(kb[i, :, cols(p)], qp[:, i * 128 : (i + 1) * 128]) for i in range(FPC)], axis=1
        )
        top = jnp.max(scores, axis=0, keepdims=True)
        weights = jnp.exp(scores - top)
        tops[p] = top
        sums[p] = jnp.sum(weights, axis=0, keepdims=True)
        weights = weights.astype(jnp.bfloat16)
        both = jnp.concatenate(
            [tn(vb[i, :, cols(p)], weights[:, i * 128 : (i + 1) * 128]) for i in range(FPC)], axis=1
        )
        acc[p] = pick_head(both)
        return carry

    pass_on(2)
    pass_on(5)
    lax.fori_loop(0, 3, own_frame, 0)
    chain_on(2)
    pass_on(3)
    pass_on(4)
    lax.fori_loop(3, PAIRS, own_frame, 0)

    for k in range(1, LEVELS + 2):
        @pl.when(z >= k)
        def _():
            ref = clips.at[LEVELS + 1 - k]
            remote(ref, ref, cz_ss.at[k], cz_rs.at[k], d).wait_recv()
    table = clips[...].reshape(8, 128)
    own_first = BASE + 4 * y
    query_clip = [
        jnp.sum(jnp.where(lane == 4 * y + i, table[LEVELS + 1 : LEVELS + 2], 0.0), axis=1, keepdims=True)
        for i in range(FPC)
    ]
    table = table.astype(jnp.bfloat16)
    ones = jnp.ones((128, 128), jnp.bfloat16)

    def key_clips(numbers, rows):
        pick = (numbers // (NY * FPC))[:, :8] == iota((rows, 8), 1)
        level = jnp.dot(pick.astype(jnp.float32).astype(jnp.bfloat16), table, preferred_element_type=jnp.float32)
        one = jnp.where(lax.rem(numbers, NY * FPC) == iota((rows, 128), 1), level, 0.0)
        return jnp.dot(one.astype(jnp.bfloat16), ones, preferred_element_type=jnp.float32)

    def far_numbers(shape):
        n = iota(shape, 0)
        at, frame = n // BLK, lax.rem(n, BLK) // FAR
        step = at + NY - 1
        col = lax.rem(step, NY)
        level = functools.reduce(
            lambda found, k: jnp.where(step // NY == ORDER.index(k) + 1, k, found), ORDER, 0
        )
        regular = (LEVELS + 1 - level) * (NY * FPC) + col * FPC + frame
        shared = jnp.where(col < y, BASE, 0) + col * FPC + frame
        held = jnp.where((at >= MIXED) & (at < MIXED + NY), shared, regular)
        return jnp.where(at == OWN, own_first + frame, held)

    def near_numbers(shape):
        return own_first - 2 + iota(shape, 0) // NEAR_ROWS

    floor = (LEVELS + 1 - z) * (NY * FPC)
    for numbers, rows, bias in ((near_numbers, NKN, bias_near), (far_numbers, NKF, bias_far)):
        number = numbers((rows, 128))
        clip_of = key_clips(number, rows)
        for i in range(FPC):
            distance = own_first + i - number
            seen = (distance >= 1) & (distance <= 2) if rows == NKN else distance > 2
            ok = seen & (number >= floor) & (clip_of == query_clip[i])
            bias[:, i * 128 : (i + 1) * 128] = jnp.where(ok, 0.0, NEG)

    @pl.when(chip > 0)
    def _():
        ref = near.at[:, pl.ds(0, 2 * NEAR_ROWS)]
        remote(ref, ref, near_ss.at[0], near_rs.at[0], d).wait_recv()

    chain_on(3)

    def level_here(k):
        @pl.when(z >= k)
        def _():
            for delta in range(1, NY):
                if not (delta == 2 and k + 1 in CHAINED):
                    came(k, delta)

    level_here(1)
    level_here(2)
    for delta in range(1, NY):
        @pl.when(y >= delta)
        def _():
            for part in range(NC):
                ref = far.at[MIXED + lax.rem(y + NY - delta, NY), part]
                remote(ref, ref, m_ss.at[delta, 0], m_rs.at[delta, part], d).wait_recv()

        @pl.when((y < delta) & (z >= LEVELS + 1))
        def _():
            came(LEVELS + 1, delta)
    ref = far.at[OWN, 1 - c]
    remote(ref, ref, own_ss.at[0], own_rs.at[0], d).wait_recv()

    theirs = pl.ds(2 * (1 - c), 2)

    def out_local(p):
        return pltpu.make_async_copy(
            ob.at[p, mine], out_hbm.at[:, :, pl.ds(pl.multiple_of(lo + p * 128, 128), 128)], o_ls.at[p]
        )

    def out_remote(p):
        return remote(
            ob.at[p, theirs], out_hbm.at[:, :, pl.ds(pl.multiple_of(lo + p * 128, 128), 128)],
            o_ss.at[p], o_rs.at[p], sibling,
        )

    def far_rows(p, first, last):
        rows = (last - first) * BLK
        both = far[first:last, :, :, cols(p)].astype(jnp.float32).reshape(rows // 8, 2, 8, 128)
        return [both[:, n].reshape(rows, 128).astype(jnp.bfloat16) for n in range(2)]

    def join(p, scores, values):
        old = tops[p]
        top = functools.reduce(jnp.maximum, [jnp.max(s, axis=0, keepdims=True) for s in scores], old)
        factor = jnp.exp(old - top)
        total = sums[p] * factor
        both = 0.0
        for s, v in zip(scores, values):
            weights = jnp.exp(s - top)
            total = total + jnp.sum(weights, axis=0, keepdims=True)
            both = both + tn(v, weights.astype(jnp.bfloat16))
        return top, total, acc[p] * factor + pick_head(both)

    def early(p, carry):
        keys, values = far_rows(p, 0, EARLY)
        scores = [nn(near[0, :NKN, cols(p)], qm[p]) + bias_near[...], nn(keys, qm[p]) + bias_far[: EARLY * BLK]]
        tops[p], sums[p], acc[p] = join(p, scores, [near[1, :NKN, cols(p)], values])
        return carry

    def late(p):
        keys, values = far_rows(p, EARLY, SLOTS)
        _, total, summed = join(p, [nn(keys, qm[p]) + bias_far[EARLY * BLK :]], [values])
        result = summed / total
        apart = jnp.concatenate(
            [jnp.where(first_head, result, 0.0), jnp.where(first_head, 0.0, result)], axis=0
        ).astype(jnp.bfloat16)
        for i in range(FPC):
            turned = apart[:, i * 128 : (i + 1) * 128].T
            ob[p, i] = turned[:TOK] + turned[TOK:]

    lax.fori_loop(0, PAIRS, early, 0)
    level_here(3)
    level_here(4)
    for group in range(0, PAIRS, 3):
        for p in range(group, group + 3):
            late(p)
        for p in range(group, group + 3):
            out_remote(p).start()
            out_local(p).start()

    for p in range(PAIRS):
        out_local(p).wait()
        out_remote(p).wait_send()
        ref = out_hbm.at[:, :, pl.ds(pl.multiple_of(hi + p * 128, 128), 128)]
        remote(ref, ref, o_ss.at[p], o_rs.at[p], sibling).wait_recv()
    for n in range(3):
        halves[n].wait_send()
    for cp in level_sends:
        cp.wait_send()
    across.wait_send()
    each_rise(lambda cp: cp.wait_send())
    each_mixed(lambda cp: cp.wait_send())

    @pl.when(z >= LEVELS + 1)
    def _():
        backward().wait_send()

    @pl.when((z >= 2) & (z < NZ - 1))
    def _():
        forward().wait_send()

    for k in CHAINED:
        @pl.when((z >= k - 1) & (z < NZ - 1))
        def _():
            chain(k).wait_send()

    for k in range(1, LEVELS + 2):
        @pl.when(z + k < NZ)
        def _():
            remote(clips.at[LEVELS + 1], clips.at[LEVELS + 1 - k], cz_ss.at[k], cz_rs.at[k], d).wait_send()

    @pl.when(chip < NZ * NY - 1)
    def _():
        near_out.wait_send()

    for k in ORDER:
        for delta in spread_to(k):
            @pl.when((z >= k) if k <= LEVELS else ((z >= k) & (y + delta >= NY)))
            def _():
                spread(k, delta).wait_send()


def on_device(queries, key_states, value_states, clip_ids):
    bf, f32 = jnp.bfloat16, jnp.float32
    dma = pltpu.SemaphoreType.DMA
    anywhere = pl.BlockSpec(memory_space=pltpu.HBM)
    return pl.pallas_call(
        kernel,
        out_shape=jax.ShapeDtypeStruct(queries.shape, bf),
        in_specs=[anywhere] * 4,
        out_specs=anywhere,
        scratch_shapes=[
            pltpu.SMEM((2,), jnp.int32),
            pltpu.VMEM((2, TOK, 2 * HALF), bf),
            pltpu.VMEM((2, TOK, 2 * HALF), bf),
            pltpu.VMEM((FPC, TOK, HALF), bf),
            pltpu.VMEM((FPC, TOK, HALF), bf),
            pltpu.VMEM((FPC, TOK, HALF), bf),
            pltpu.VMEM((2, BLK, HALF), bf),
            pltpu.VMEM((SLOTS, NC, BLK, HALF), bf),
            pltpu.VMEM((2, 6 * NEAR_ROWS, HALF), bf),
            pltpu.VMEM((PAIRS, 128, LANES), bf),
            pltpu.VMEM((NY * NC, 1, 128), f32),
            pltpu.VMEM((8, 1, 128), f32),
            pltpu.VMEM((NKF, LANES), f32),
            pltpu.VMEM((NKN, LANES), f32),
            pltpu.VMEM((PAIRS, HEAD_DIM, LANES), f32),
            pltpu.VMEM((PAIRS, 1, LANES), f32),
            pltpu.VMEM((PAIRS, 1, LANES), f32),
            pltpu.VMEM((PAIRS, FPC, TOK, 128), bf),
            dma((6,)),
            dma((3,)), dma((3,)),
            dma((1,)), dma((1,)),
            dma((LEVELS + 2, NC)), dma((LEVELS + 2, NC)),
            dma((NY, NC)), dma((NY, NC)),
            dma((LEVELS + 2, NY)), dma((LEVELS + 2, NY)), dma((LEVELS + 2,)),
            dma((1,)), dma((1,)),
            dma((NY * NC,)), dma((NY * NC,)),
            dma((LEVELS + 2,)), dma((LEVELS + 2,)),
            dma((PAIRS,)), dma((PAIRS,)), dma((PAIRS,)),
        ],
        compiler_params=pltpu.CompilerParams(
            collective_id=0, has_side_effects=True, vmem_limit_bytes=64 << 20
        ),
        cost_estimate=pl.CostEstimate(flops=1 << 30, bytes_accessed=4 << 20, transcendentals=1 << 21),
    )(queries, key_states, value_states, clip_ids)


def solution(mesh):
    frames = P(("dp", "tm"), None, None)
    return jax.shard_map(
        on_device,
        mesh=mesh,
        in_specs=(frames, frames, frames, P(("dp", "tm"))),
        out_specs=frames,
        check_vma=False,
    )
```

```python
import functools

import jax
import jax.numpy as jnp
from jax import lax
from jax.experimental import pallas as pl
from jax.experimental.pallas import tpu as pltpu
from jax.sharding import PartitionSpec as P

HEAD_DIM = 64
SIDE = 8
TOK = 64
NZ, NY, NC = 8, 4, 2
FPC = 4
HALF = 768
PAIRS = HALF // 128
ROWS = FPC * TOK
LANES = 2 * ROWS
FAR = 4
BLK = FPC * FAR
LEVELS = 4
OWN = 0
ORDER = (1, 2, 5, 3, 4)
FIRST = {k: 1 + n * NY for n, k in enumerate(ORDER)}
DIRECT = (1, 2, 5)
CHAINED = (2,)
MIXED = FIRST[LEVELS + 1]
SLOTS = 1 + 5 * NY
CHUNKS = (FIRST[2], FIRST[3])
NKF = SLOTS * BLK
NEAR_ROWS = 16
NKN = 5 * NEAR_ROWS
FLAT = (LEVELS + 2) * NY * FPC
BASE = FLAT - NY * FPC
NEG = -1e30
MESH = pl.DeviceIdType.MESH


def iota(shape, dim):
    return lax.broadcasted_iota(jnp.int32, shape, dim)


def remote(src, dst, ss, rs, to):
    return pltpu.make_async_remote_copy(
        src_ref=src, dst_ref=dst, send_sem=ss, recv_sem=rs, device_id={"tm": to}, device_id_type=MESH
    )


def nt(a, b):
    return lax.dot_general(a, b, (((1,), (1,)), ((), ())), preferred_element_type=jnp.float32)


def nn(a, b):
    return jnp.dot(a, b, preferred_element_type=jnp.float32)


def tn(a, b):
    return lax.dot_general(a, b, (((0,), (0,)), ((), ())), preferred_element_type=jnp.float32)


def kernel(
    q_hbm, k_hbm, v_hbm, clip_hbm, out_hbm,
    clip_ref, kf, vf, qb, kb, vb, pooled, far, near, qm, level_clips, clips, bias_far, bias_near, acc, tops, sums, ob,
    in_sem, sib_ss, sib_rs, own_ss, own_rs, z_ss, z_rs, m_ss, m_rs, y_ss, y_rs, x_ss,
    near_ss, near_rs, cy_ss, cy_rs, cz_ss, cz_rs, o_ss, o_rs, o_ls,
):
    d = lax.axis_index("tm")
    z, y, c = d // (NY * NC), lax.rem(d // NC, NY), lax.rem(d, NC)
    chip = d // NC

    def dev(zz, yy, cc):
        return zz * (NY * NC) + yy * NC + cc

    sibling = dev(z, y, 1 - c)

    barrier = pltpu.get_barrier_semaphore()

    def greet(to):
        pl.semaphore_signal(barrier, inc=1, device_id={"tm": to}, device_id_type=MESH)

    for k in range(LEVELS + 1, 0, -1):
        @pl.when(z >= k)
        def _():
            greet(dev(z - k, y, c))
            if k in DIRECT:
                greet(dev(z - k, y, 1 - c))

    last_rise = NZ - 1 - LEVELS

    @pl.when(z == NZ - 1)
    def _():
        greet(dev(last_rise, y, 1 - c))

    @pl.when((y == 0) & (z > 0))
    def _():
        greet(dev(z - 1, NY - 1, c))

    for yy in range(1, NY):
        for cc in range(NC):
            greet(dev(z, lax.rem(y + yy, NY), cc))
    greet(sibling)

    lo = pl.multiple_of(c * HALF, 128)
    hi = pl.multiple_of((1 - c) * HALF, 128)
    mine = pl.ds(2 * c, 2)
    whole = []
    for n, (src, dst) in enumerate(((k_hbm, kf), (v_hbm, vf))):
        cp = pltpu.make_async_copy(src, dst, in_sem.at[n])
        cp.start()
        whole.append(cp)
    clip_copy = pltpu.make_async_copy(clip_hbm, clip_ref, in_sem.at[2])
    clip_copy.start()
    local = []
    for n, (src, dst) in enumerate(((k_hbm, kb), (v_hbm, vb), (q_hbm, qb))):
        cp = pltpu.make_async_copy(src.at[:, :, pl.ds(lo, HALF)], dst.at[mine], in_sem.at[3 + n])
        cp.start()
        local.append(cp)

    for k in ORDER:
        for col in range(NY):
            @pl.when((z < k) & (col >= y) if k == LEVELS + 1 else z < k)
            def _():
                far[FIRST[k] + col] = jnp.zeros(far.shape[1:], far.dtype)

    @pl.when(chip == 0)
    def _():
        near[:, : 2 * NEAR_ROWS] = jnp.zeros((2, 2 * NEAR_ROWS, HALF), jnp.bfloat16)

    for k in range(1, LEVELS + 2):
        @pl.when(z < k)
        def _():
            clips[LEVELS + 1 - k] = jnp.zeros((1, 128), jnp.float32)
    for n in range(LEVELS + 2, 8):
        clips[n] = jnp.zeros((1, 128), jnp.float32)

    def pool_matrix(rows, frames, side):
        r, t = iota((rows, frames * TOK), 0), iota((rows, frames * TOK), 1)
        frame, token = t // TOK, lax.rem(t, TOK)
        cells = SIDE // side
        at = frame * cells * cells + (token // SIDE // side) * cells + lax.rem(token, SIDE) // side
        return jnp.where(r == at, 1.0 / (side * side), 0.0).astype(jnp.bfloat16)

    far_pool = pool_matrix(2 * FAR, 2, 4)
    means = []
    for n, full in enumerate((kf, vf)):
        whole[n].wait()
        means.append(nn(far_pool, full[...].reshape(2 * TOK, 2 * HALF)))
    means = jnp.concatenate(means, axis=0).astype(jnp.bfloat16)
    for n in range(2):
        pooled[n] = means[:, n * HALF : (n + 1) * HALF]

    up = jnp.minimum(NZ - 1 - z, LEVELS + 1)
    crossing = sum(jnp.where(z + k < NZ, 1, 0) for k in DIRECT) + jnp.where(z == last_rise, 1, 0)
    next_near = jnp.where((y == NY - 1) & (z < NZ - 1), 1, 0)
    pl.semaphore_wait(barrier, (NY - 1) * NC + 1 + up + crossing + next_near)

    def slot(k, col):
        return FIRST[k] + col

    def rise(k, core):
        return remote(
            pooled.at[core], far.at[slot(k, y), c], z_ss.at[k, core], z_rs.at[k, c], dev(z + k, y, core)
        )

    def mixed(delta, core):
        return remote(
            pooled.at[core], far.at[MIXED + y, c], m_ss.at[delta, core], m_rs.at[delta, c],
            dev(z, lax.rem(y + delta, NY), core),
        )

    def each_rise(act):
        for k in DIRECT:
            @pl.when(z + k < NZ)
            def _():
                for core in range(NC):
                    act(rise(k, core))

        @pl.when(z == last_rise)
        def _():
            for core in range(NC):
                act(rise(LEVELS, core))

    def each_mixed(act):
        for delta in (1, 3, 2):
            @pl.when(y + delta < NY)
            def _():
                for core in range(NC):
                    act(mixed(delta, core))

    each_rise(lambda cp: cp.start())
    each_mixed(lambda cp: cp.start())
    across = remote(pooled.at[1 - c], far.at[OWN, c], own_ss.at[0], own_rs.at[0], sibling)
    across.start()
    far[OWN, c] = pooled[c]

    halves = []
    for n, (src, dst) in enumerate(((k_hbm, kb), (v_hbm, vb), (q_hbm, qb))):
        cp = remote(src.at[:, :, pl.ds(hi, HALF)], dst.at[mine], sib_ss.at[n], sib_rs.at[n], sibling)
        cp.start()
        halves.append(cp)

    def wait_half(n):
        local[n].wait()
        other = (kb, vb, qb)[n].at[pl.ds(2 * (1 - c), 2)]
        remote(other, other, sib_ss.at[n], sib_rs.at[n], sibling).wait_recv()

    clip_copy.wait()
    row = y * NC + c
    lane = iota((1, 128), 1)
    level_clips[row] = sum(
        jnp.where(lane == 2 * row + n, clip_ref[n].astype(jnp.float32), 0.0) for n in range(2)
    )
    level_sends = []
    for n in range(1, NY * NC):
        to = lax.rem(row + n, NY * NC)
        ref = level_clips.at[row]
        cp = remote(ref, ref, cy_ss.at[n], cy_rs.at[n], z * (NY * NC) + to)
        cp.start()
        level_sends.append(cp)

    near_pool = pool_matrix(NEAR_ROWS * FPC, FPC, 2)
    for n, full in enumerate((kb, vb)):
        wait_half(n)
        near[n, 2 * NEAR_ROWS :] = nn(near_pool, full[...].reshape(ROWS, HALF)).astype(jnp.bfloat16)

    near_out = remote(
        near.at[:, pl.ds(4 * NEAR_ROWS, 2 * NEAR_ROWS)], near.at[:, pl.ds(0, 2 * NEAR_ROWS)],
        near_ss.at[0], near_rs.at[0], jnp.minimum((chip + 1) * NC + c, NZ * NY * NC - 1),
    )

    @pl.when(chip < NZ * NY - 1)
    def _():
        near_out.start()

    for n in range(1, NY * NC):
        ref = level_clips.at[lax.rem(row + NY * NC - n, NY * NC)]
        remote(ref, ref, cy_ss.at[n], cy_rs.at[n], d).wait_recv()
    clips[LEVELS + 1] = jnp.sum(level_clips[...], axis=0)
    for k in range(1, LEVELS + 2):
        @pl.when(z + k < NZ)
        def _():
            remote(
                clips.at[LEVELS + 1], clips.at[LEVELS + 1 - k], cz_ss.at[k], cz_rs.at[k], dev(z + k, y, c)
            ).start()

    def spread(k, delta):
        ref = far.at[slot(k, y)]
        return remote(ref, ref, y_ss.at[k, delta], y_rs.at[k, delta], dev(z, lax.rem(y + delta, NY), c))

    def arrived(k, part):
        ref = far.at[slot(k, y), part]
        remote(ref, ref, z_ss.at[k, 0], z_rs.at[k, part], d).wait_recv()

    def arrived_whole(k):
        ref = far.at[slot(k, y)]
        remote(ref, ref, z_ss.at[k, 0], z_rs.at[k, 0], d).wait_recv()

    def forward():
        return remote(far.at[slot(2, y)], far.at[slot(3, y)], z_ss.at[3, 0], z_rs.at[3, 0], dev(z + 1, y, c))

    def backward():
        return remote(far.at[slot(5, y)], far.at[slot(4, y)], z_ss.at[4, 0], z_rs.at[4, 0], dev(z - 1, y, c))

    def spread_to(k):
        return (1, 3) if k in CHAINED else (2, 1, 3)

    def pass_on(k):
        @pl.when(z >= k)
        def _():
            if k in DIRECT:
                for part in range(NC):
                    arrived(k, part)
            elif k == LEVELS:
                @pl.when(z == NZ - 1)
                def _():
                    for part in range(NC):
                        arrived(k, part)

                @pl.when(z < NZ - 1)
                def _():
                    arrived_whole(k)
            else:
                arrived_whole(k)
            if k == 2:
                @pl.when(z < NZ - 1)
                def _():
                    forward().start()
            if k == LEVELS + 1:
                backward().start()
            for delta in spread_to(k):
                if k <= LEVELS:
                    spread(k, delta).start()
                else:
                    @pl.when(y + delta >= NY)
                    def _():
                        spread(k, delta).start()

    opposite = lax.rem(y + 2, NY)

    def chain(k):
        return remote(
            far.at[slot(k - 1, opposite)], far.at[slot(k, opposite)], x_ss.at[k], y_rs.at[k, 2], dev(z + 1, y, c)
        )

    def came(k, delta):
        ref = far.at[slot(k, lax.rem(y + NY - delta, NY))]
        remote(ref, ref, y_ss.at[k, delta], y_rs.at[k, delta], d).wait_recv()

    def chain_on(k):
        if k not in CHAINED:
            return

        @pl.when(z >= k - 1)
        def _():
            came(k - 1, 2)

            @pl.when(z < NZ - 1)
            def _():
                chain(k).start()

    pass_on(1)

    wait_half(2)

    def cols(p):
        return pl.ds(pl.multiple_of(p * 128, 128), 128)

    def lanes(head, group):
        return slice(head * ROWS + group * 128, head * ROWS + (group + 1) * 128)

    first_rows = iota((128, 128), 0) < HEAD_DIM
    nothing = jnp.zeros((128, 128), jnp.bfloat16)
    for p in range(PAIRS):
        for group in range(2):
            part = qb[2 * group : 2 * group + 2, :, p * 128 : (p + 1) * 128].reshape(128, 128)
            turned = (part * jnp.bfloat16(HEAD_DIM ** -0.5)).T
            qm[p, :, lanes(0, group)] = jnp.where(first_rows, turned, nothing)
            qm[p, :, lanes(1, group)] = jnp.where(first_rows, nothing, turned)

    first_frame = iota((1, 128), 1) < TOK

    def own_frame(p, carry):
        def two_frames(ref, group):
            return ref[2 * group : 2 * group + 2, :, cols(p)].reshape(128, 128)

        keys = [two_frames(kb, group) for group in range(2)]
        values = [two_frames(vb, group) for group in range(2)]
        scores = []
        for head in range(2):
            for group in range(2):
                both = nn(keys[group], qm[p, :, lanes(head, group)])
                scores.append(jnp.where(first_frame, both[:TOK], both[TOK:]))
        scores = jnp.concatenate(scores, axis=1)
        top = jnp.max(scores, axis=0, keepdims=True)
        weights = jnp.exp(scores - top)
        tops[p] = top
        sums[p] = jnp.sum(weights, axis=0, keepdims=True)
        for head in range(2):
            for group in range(2):
                part = weights[:, lanes(head, group)]
                apart = jnp.concatenate(
                    [jnp.where(first_frame, part, 0.0), jnp.where(first_frame, 0.0, part)], axis=0
                ).astype(jnp.bfloat16)
                acc[p, :, lanes(head, group)] = tn(values[group], apart)[head * HEAD_DIM : (head + 1) * HEAD_DIM]
        return carry

    pass_on(2)
    pass_on(5)
    lax.fori_loop(0, 3, own_frame, 0, unroll=3)
    chain_on(2)
    pass_on(3)
    pass_on(4)
    lax.fori_loop(3, PAIRS, own_frame, 0, unroll=3)

    for k in range(1, LEVELS + 2):
        @pl.when(z >= k)
        def _():
            ref = clips.at[LEVELS + 1 - k]
            remote(ref, ref, cz_ss.at[k], cz_rs.at[k], d).wait_recv()
    table = clips[...].reshape(8, 128)
    own_first = BASE + 4 * y
    query_clip = [
        jnp.sum(jnp.where(lane == 4 * y + i, table[LEVELS + 1 : LEVELS + 2], 0.0), axis=1, keepdims=True)
        for i in range(FPC)
    ]
    table = table.astype(jnp.bfloat16)
    ones = jnp.ones((128, 128), jnp.bfloat16)

    def key_clips(numbers, rows):
        pick = (numbers // (NY * FPC))[:, :8] == iota((rows, 8), 1)
        level = jnp.dot(pick.astype(jnp.float32).astype(jnp.bfloat16), table, preferred_element_type=jnp.float32)
        one = jnp.where(lax.rem(numbers, NY * FPC) == iota((rows, 128), 1), level, 0.0)
        return jnp.dot(one.astype(jnp.bfloat16), ones, preferred_element_type=jnp.float32)

    def far_numbers(shape):
        n = iota(shape, 0)
        at, frame = n // BLK, lax.rem(n, BLK) // FAR
        step = at + NY - 1
        col = lax.rem(step, NY)
        level = functools.reduce(
            lambda found, k: jnp.where(step // NY == ORDER.index(k) + 1, k, found), ORDER, 0
        )
        regular = (LEVELS + 1 - level) * (NY * FPC) + col * FPC + frame
        shared = jnp.where(col < y, BASE, 0) + col * FPC + frame
        held = jnp.where((at >= MIXED) & (at < MIXED + NY), shared, regular)
        return jnp.where(at == OWN, own_first + frame, held)

    def near_numbers(shape):
        return own_first - 2 + iota(shape, 0) // NEAR_ROWS

    floor = (LEVELS + 1 - z) * (NY * FPC)
    for numbers, rows, bias in ((near_numbers, NKN, bias_near), (far_numbers, NKF, bias_far)):
        number = numbers((rows, 128))
        clip_of = key_clips(number, rows)
        for group in range(2):
            distance = own_first + 2 * group + lane // TOK - number
            seen = (distance >= 1) & (distance <= 2) if rows == NKN else distance > 2
            clip_here = jnp.where(first_frame, query_clip[2 * group], query_clip[2 * group + 1])
            ok = seen & (number >= floor) & (clip_of == clip_here)
            bias[:, group * 128 : (group + 1) * 128] = jnp.where(ok, 0.0, NEG)

    @pl.when(chip > 0)
    def _():
        ref = near.at[:, pl.ds(0, 2 * NEAR_ROWS)]
        remote(ref, ref, near_ss.at[0], near_rs.at[0], d).wait_recv()

    chain_on(3)

    def level_here(k):
        @pl.when(z >= k)
        def _():
            for delta in range(1, NY):
                if not (delta == 2 and k + 1 in CHAINED):
                    came(k, delta)

    def shared_here():
        for delta in range(1, NY):
            @pl.when(y >= delta)
            def _():
                for part in range(NC):
                    ref = far.at[MIXED + lax.rem(y + NY - delta, NY), part]
                    remote(ref, ref, m_ss.at[delta, 0], m_rs.at[delta, part], d).wait_recv()

            @pl.when((y < delta) & (z >= LEVELS + 1))
            def _():
                came(LEVELS + 1, delta)

    ref = far.at[OWN, 1 - c]
    remote(ref, ref, own_ss.at[0], own_rs.at[0], d).wait_recv()

    theirs = pl.ds(2 * (1 - c), 2)

    def out_local(p):
        return pltpu.make_async_copy(
            ob.at[p, mine], out_hbm.at[:, :, pl.ds(pl.multiple_of(lo + p * 128, 128), 128)], o_ls.at[p]
        )

    def out_remote(p):
        return remote(
            ob.at[p, theirs], out_hbm.at[:, :, pl.ds(pl.multiple_of(lo + p * 128, 128), 128)],
            o_ss.at[p], o_rs.at[p], sibling,
        )

    def far_rows(p, first, last):
        rows = (last - first) * BLK
        both = far[first:last, :, :, cols(p)].astype(jnp.float32).reshape(rows // 8, 2, 8, 128)
        return [both[:, n].reshape(rows, 128).astype(jnp.bfloat16) for n in range(2)]

    def join(p, keys, values, bias):
        scores = nn(keys, qm[p]) + jnp.concatenate([bias, bias], axis=1)
        old = tops[p]
        top = jnp.maximum(old, jnp.max(scores, axis=0, keepdims=True))
        factor = jnp.exp(old - top)
        weights = jnp.exp(scores - top)
        total = sums[p] * factor + jnp.sum(weights, axis=0, keepdims=True)
        weights = weights.astype(jnp.bfloat16)
        turned = values.T
        summed = [
            nn(turned[n * HEAD_DIM : (n + 1) * HEAD_DIM], weights[:, n * ROWS : (n + 1) * ROWS]) for n in range(2)
        ]
        return top, total, acc[p] * factor + jnp.concatenate(summed, axis=1)

    def keep(part):
        joined = [join(p, *part(p)) for p in range(PAIRS)]
        for p, (top, total, summed) in enumerate(joined):
            tops[p], sums[p], acc[p] = top, total, summed

    def nearest(p):
        keys, values = far_rows(p, 0, CHUNKS[0])
        keys = jnp.concatenate([near[0, :NKN, cols(p)], keys], axis=0)
        values = jnp.concatenate([near[1, :NKN, cols(p)], values], axis=0)
        return keys, values, jnp.concatenate([bias_near[...], bias_far[: CHUNKS[0] * BLK]], axis=0)

    def middle(p):
        return *far_rows(p, *CHUNKS), bias_far[CHUNKS[0] * BLK : CHUNKS[1] * BLK]

    def put(p, total, summed):
        result = (summed / total).astype(jnp.bfloat16)
        for group in range(2):
            turned = jnp.concatenate([result[:, lanes(head, group)] for head in range(2)], axis=0).T
            ob[p, 2 * group] = turned[:TOK]
            ob[p, 2 * group + 1] = turned[TOK:]

    level_here(1)
    keep(nearest)
    level_here(2)
    shared_here()
    keep(middle)
    level_here(3)
    level_here(4)
    def send_out(group):
        for p in group:
            out_remote(p).start()
            out_local(p).start()

    groups = (range(0, 3), range(3, PAIRS))

    @pl.when(z >= 3)
    def _():
        for group in groups:
            for p in group:
                put(p, *join(p, *far_rows(p, CHUNKS[1], SLOTS), bias_far[CHUNKS[1] * BLK :])[1:])
            send_out(group)

    @pl.when(z < 3)
    def _():
        for group in groups:
            for p in group:
                put(p, sums[p], acc[p])
            send_out(group)

    for p in range(PAIRS):
        out_local(p).wait()
        out_remote(p).wait_send()
        ref = out_hbm.at[:, :, pl.ds(pl.multiple_of(hi + p * 128, 128), 128)]
        remote(ref, ref, o_ss.at[p], o_rs.at[p], sibling).wait_recv()
    for n in range(3):
        halves[n].wait_send()
    for cp in level_sends:
        cp.wait_send()
    across.wait_send()
    each_rise(lambda cp: cp.wait_send())
    each_mixed(lambda cp: cp.wait_send())

    @pl.when(z >= LEVELS + 1)
    def _():
        backward().wait_send()

    @pl.when((z >= 2) & (z < NZ - 1))
    def _():
        forward().wait_send()

    for k in CHAINED:
        @pl.when((z >= k - 1) & (z < NZ - 1))
        def _():
            chain(k).wait_send()

    for k in range(1, LEVELS + 2):
        @pl.when(z + k < NZ)
        def _():
            remote(clips.at[LEVELS + 1], clips.at[LEVELS + 1 - k], cz_ss.at[k], cz_rs.at[k], d).wait_send()

    @pl.when(chip < NZ * NY - 1)
    def _():
        near_out.wait_send()

    for k in ORDER:
        for delta in spread_to(k):
            @pl.when((z >= k) if k <= LEVELS else ((z >= k) & (y + delta >= NY)))
            def _():
                spread(k, delta).wait_send()


def on_device(queries, key_states, value_states, clip_ids):
    bf, f32 = jnp.bfloat16, jnp.float32
    dma = pltpu.SemaphoreType.DMA
    anywhere = pl.BlockSpec(memory_space=pltpu.HBM)
    return pl.pallas_call(
        kernel,
        out_shape=jax.ShapeDtypeStruct(queries.shape, bf),
        in_specs=[anywhere] * 4,
        out_specs=anywhere,
        scratch_shapes=[
            pltpu.SMEM((2,), jnp.int32),
            pltpu.VMEM((2, TOK, 2 * HALF), bf),
            pltpu.VMEM((2, TOK, 2 * HALF), bf),
            pltpu.VMEM((FPC, TOK, HALF), bf),
            pltpu.VMEM((FPC, TOK, HALF), bf),
            pltpu.VMEM((FPC, TOK, HALF), bf),
            pltpu.VMEM((2, BLK, HALF), bf),
            pltpu.VMEM((SLOTS, NC, BLK, HALF), bf),
            pltpu.VMEM((2, 6 * NEAR_ROWS, HALF), bf),
            pltpu.VMEM((PAIRS, 128, LANES), bf),
            pltpu.VMEM((NY * NC, 1, 128), f32),
            pltpu.VMEM((8, 1, 128), f32),
            pltpu.VMEM((NKF, ROWS), f32),
            pltpu.VMEM((NKN, ROWS), f32),
            pltpu.VMEM((PAIRS, HEAD_DIM, LANES), f32),
            pltpu.VMEM((PAIRS, 1, LANES), f32),
            pltpu.VMEM((PAIRS, 1, LANES), f32),
            pltpu.VMEM((PAIRS, FPC, TOK, 128), bf),
            dma((6,)),
            dma((3,)), dma((3,)),
            dma((1,)), dma((1,)),
            dma((LEVELS + 2, NC)), dma((LEVELS + 2, NC)),
            dma((NY, NC)), dma((NY, NC)),
            dma((LEVELS + 2, NY)), dma((LEVELS + 2, NY)), dma((LEVELS + 2,)),
            dma((1,)), dma((1,)),
            dma((NY * NC,)), dma((NY * NC,)),
            dma((LEVELS + 2,)), dma((LEVELS + 2,)),
            dma((PAIRS,)), dma((PAIRS,)), dma((PAIRS,)),
        ],
        compiler_params=pltpu.CompilerParams(
            collective_id=0, has_side_effects=True, vmem_limit_bytes=64 << 20
        ),
        cost_estimate=pl.CostEstimate(flops=1 << 30, bytes_accessed=4 << 20, transcendentals=1 << 21),
    )(queries, key_states, value_states, clip_ids)


def solution(mesh):
    frames = P(("dp", "tm"), None, None)
    return jax.shard_map(
        on_device,
        mesh=mesh,
        in_specs=(frames, frames, frames, P(("dp", "tm"))),
        out_specs=frames,
        check_vma=False,
    )
```

```python
import functools

import jax
import jax.numpy as jnp
from jax import lax
from jax.experimental import pallas as pl
from jax.experimental.pallas import tpu as pltpu
from jax.sharding import PartitionSpec as P

HEAD_DIM = 64
SIDE = 8
TOK = 64
NZ, NY, NC = 8, 4, 2
FPC = 4
HALF = 768
PAIRS = HALF // 128
ROWS = FPC * TOK
LANES = 2 * ROWS
FAR = 4
BLK = FPC * FAR
LEVELS = 4
OWN = 0
ORDER = (1, 2, 5, 3, 4)
FIRST = {k: 1 + n * NY for n, k in enumerate(ORDER)}
DIRECT = (1, 2, 5)
HALVED = (3, 4)
CHAINED = (2,)
MIXED = FIRST[LEVELS + 1]
SLOTS = 1 + 5 * NY
CHUNKS = (FIRST[2], FIRST[3])
NKF = SLOTS * BLK
NEAR_ROWS = 16
NKN = 5 * NEAR_ROWS
FLAT = (LEVELS + 2) * NY * FPC
BASE = FLAT - NY * FPC
NEG = -1e30
MESH = pl.DeviceIdType.MESH


def iota(shape, dim):
    return lax.broadcasted_iota(jnp.int32, shape, dim)


def remote(src, dst, ss, rs, to):
    return pltpu.make_async_remote_copy(
        src_ref=src, dst_ref=dst, send_sem=ss, recv_sem=rs, device_id={"tm": to}, device_id_type=MESH
    )


def nt(a, b):
    return lax.dot_general(a, b, (((1,), (1,)), ((), ())), preferred_element_type=jnp.float32)


def nn(a, b):
    return jnp.dot(a, b, preferred_element_type=jnp.float32)


def tn(a, b):
    return lax.dot_general(a, b, (((0,), (0,)), ((), ())), preferred_element_type=jnp.float32)


def kernel(
    q_hbm, k_hbm, v_hbm, clip_hbm, out_hbm,
    clip_ref, kf, vf, qb, kb, vb, pooled, far, near, qm, level_clips, clips, bias_far, bias_near, acc, tops, sums, ob,
    in_sem, sib_ss, sib_rs, own_ss, own_rs, z_ss, z_rs, m_ss, m_rs, y_ss, y_rs, x_ss,
    near_ss, near_rs, cy_ss, cy_rs, cz_ss, cz_rs, o_ss, o_rs, o_ls,
):
    d = lax.axis_index("tm")
    z, y, c = d // (NY * NC), lax.rem(d // NC, NY), lax.rem(d, NC)
    chip = d // NC

    def dev(zz, yy, cc):
        return zz * (NY * NC) + yy * NC + cc

    sibling = dev(z, y, 1 - c)

    barrier = pltpu.get_barrier_semaphore()

    def greet(to):
        pl.semaphore_signal(barrier, inc=1, device_id={"tm": to}, device_id_type=MESH)

    for k in range(LEVELS + 1, 0, -1):
        @pl.when(z >= k)
        def _():
            greet(dev(z - k, y, c))
            if k in DIRECT:
                greet(dev(z - k, y, 1 - c))

    last_rise = NZ - 1 - LEVELS

    @pl.when(z == NZ - 1)
    def _():
        greet(dev(last_rise, y, 1 - c))

    @pl.when((y == 0) & (z > 0))
    def _():
        greet(dev(z - 1, NY - 1, c))

    for yy in range(1, NY):
        for cc in range(NC):
            greet(dev(z, lax.rem(y + yy, NY), cc))
    greet(sibling)

    lo = pl.multiple_of(c * HALF, 128)
    hi = pl.multiple_of((1 - c) * HALF, 128)
    mine = pl.ds(2 * c, 2)
    whole = []
    for n, (src, dst) in enumerate(((k_hbm, kf), (v_hbm, vf))):
        cp = pltpu.make_async_copy(src, dst, in_sem.at[n])
        cp.start()
        whole.append(cp)
    clip_copy = pltpu.make_async_copy(clip_hbm, clip_ref, in_sem.at[2])
    clip_copy.start()
    local = []
    for n, (src, dst) in enumerate(((k_hbm, kb), (v_hbm, vb), (q_hbm, qb))):
        cp = pltpu.make_async_copy(src.at[:, :, pl.ds(lo, HALF)], dst.at[mine], in_sem.at[3 + n])
        cp.start()
        local.append(cp)

    for k in ORDER:
        for col in range(NY):
            @pl.when((z < k) & (col >= y) if k == LEVELS + 1 else z < k)
            def _():
                far[FIRST[k] + col] = jnp.zeros(far.shape[1:], far.dtype)

    @pl.when(chip == 0)
    def _():
        near[:, : 2 * NEAR_ROWS] = jnp.zeros((2, 2 * NEAR_ROWS, HALF), jnp.bfloat16)

    for k in range(1, LEVELS + 2):
        @pl.when(z < k)
        def _():
            clips[LEVELS + 1 - k] = jnp.zeros((1, 128), jnp.float32)
    for n in range(LEVELS + 2, 8):
        clips[n] = jnp.zeros((1, 128), jnp.float32)

    def pool_matrix(rows, frames, side):
        r, t = iota((rows, frames * TOK), 0), iota((rows, frames * TOK), 1)
        frame, token = t // TOK, lax.rem(t, TOK)
        cells = SIDE // side
        at = frame * cells * cells + (token // SIDE // side) * cells + lax.rem(token, SIDE) // side
        return jnp.where(r == at, 1.0 / (side * side), 0.0).astype(jnp.bfloat16)

    far_pool = pool_matrix(2 * FAR, 2, 4)
    means = []
    for n, full in enumerate((kf, vf)):
        whole[n].wait()
        means.append(nn(far_pool, full[...].reshape(2 * TOK, 2 * HALF)))
    means = jnp.concatenate(means, axis=0).astype(jnp.bfloat16)
    for n in range(2):
        pooled[n] = means[:, n * HALF : (n + 1) * HALF]

    up = jnp.minimum(NZ - 1 - z, LEVELS + 1)
    crossing = sum(jnp.where(z + k < NZ, 1, 0) for k in DIRECT) + jnp.where(z == last_rise, 1, 0)
    next_near = jnp.where((y == NY - 1) & (z < NZ - 1), 1, 0)
    pl.semaphore_wait(barrier, (NY - 1) * NC + 1 + up + crossing + next_near)

    def slot(k, col):
        return FIRST[k] + col

    def rise(k, core):
        return remote(
            pooled.at[core], far.at[slot(k, y), c], z_ss.at[k, core], z_rs.at[k, c], dev(z + k, y, core)
        )

    def mixed(delta, core):
        return remote(
            pooled.at[core], far.at[MIXED + y, c], m_ss.at[delta, core], m_rs.at[delta, c],
            dev(z, lax.rem(y + delta, NY), core),
        )

    def each_rise(act):
        for k in DIRECT:
            @pl.when(z + k < NZ)
            def _():
                for core in range(NC):
                    act(rise(k, core))

        @pl.when(z == last_rise)
        def _():
            for core in range(NC):
                act(rise(LEVELS, core))

    def each_mixed(act):
        for delta in (1, 3, 2):
            @pl.when(y + delta < NY)
            def _():
                for core in range(NC):
                    act(mixed(delta, core))

    each_rise(lambda cp: cp.start())
    each_mixed(lambda cp: cp.start())
    across = remote(pooled.at[1 - c], far.at[OWN, c], own_ss.at[0], own_rs.at[0], sibling)
    across.start()
    far[OWN, c] = pooled[c]

    halves = []
    for n, (src, dst) in enumerate(((k_hbm, kb), (v_hbm, vb), (q_hbm, qb))):
        cp = remote(src.at[:, :, pl.ds(hi, HALF)], dst.at[mine], sib_ss.at[n], sib_rs.at[n], sibling)
        cp.start()
        halves.append(cp)

    def wait_half(n):
        local[n].wait()
        other = (kb, vb, qb)[n].at[pl.ds(2 * (1 - c), 2)]
        remote(other, other, sib_ss.at[n], sib_rs.at[n], sibling).wait_recv()

    clip_copy.wait()
    row = y * NC + c
    lane = iota((1, 128), 1)
    level_clips[row] = sum(
        jnp.where(lane == 2 * row + n, clip_ref[n].astype(jnp.float32), 0.0) for n in range(2)
    )
    level_sends = []
    for n in range(1, NY * NC):
        to = lax.rem(row + n, NY * NC)
        ref = level_clips.at[row]
        cp = remote(ref, ref, cy_ss.at[n], cy_rs.at[n], z * (NY * NC) + to)
        cp.start()
        level_sends.append(cp)

    near_pool = pool_matrix(NEAR_ROWS * FPC, FPC, 2)
    for n, full in enumerate((kb, vb)):
        wait_half(n)
        near[n, 2 * NEAR_ROWS :] = nn(near_pool, full[...].reshape(ROWS, HALF)).astype(jnp.bfloat16)

    near_out = remote(
        near.at[:, pl.ds(4 * NEAR_ROWS, 2 * NEAR_ROWS)], near.at[:, pl.ds(0, 2 * NEAR_ROWS)],
        near_ss.at[0], near_rs.at[0], jnp.minimum((chip + 1) * NC + c, NZ * NY * NC - 1),
    )

    @pl.when(chip < NZ * NY - 1)
    def _():
        near_out.start()

    for n in range(1, NY * NC):
        ref = level_clips.at[lax.rem(row + NY * NC - n, NY * NC)]
        remote(ref, ref, cy_ss.at[n], cy_rs.at[n], d).wait_recv()
    clips[LEVELS + 1] = jnp.sum(level_clips[...], axis=0)
    for k in range(1, LEVELS + 2):
        @pl.when(z + k < NZ)
        def _():
            remote(
                clips.at[LEVELS + 1], clips.at[LEVELS + 1 - k], cz_ss.at[k], cz_rs.at[k], dev(z + k, y, c)
            ).start()

    def spread(k, delta, half=None):
        ref, at = whole_or_half(slot(k, y), half), delta + NY * (half or 0)
        return remote(ref, ref, y_ss.at[k, at], y_rs.at[k, at], dev(z, lax.rem(y + delta, NY), c))

    def whole_or_half(at, half):
        if half is None:
            return far.at[at]
        return far.at[at, :, :, half * (HALF // 2) : (half + 1) * (HALF // 2)]

    def arrived(k, part):
        ref = far.at[slot(k, y), part]
        remote(ref, ref, z_ss.at[k, 0], z_rs.at[k, part], d).wait_recv()

    def arrived_whole(k):
        ref = far.at[slot(k, y)]
        remote(ref, ref, z_ss.at[k, 0], z_rs.at[k, 0], d).wait_recv()

    def forward():
        return remote(far.at[slot(2, y)], far.at[slot(3, y)], z_ss.at[3, 0], z_rs.at[3, 0], dev(z + 1, y, c))

    def backward():
        return remote(far.at[slot(5, y)], far.at[slot(4, y)], z_ss.at[4, 0], z_rs.at[4, 0], dev(z - 1, y, c))

    def spread_to(k):
        return (1, 3) if k in CHAINED else (2, 1, 3)

    def pass_on(k):
        @pl.when(z >= k)
        def _():
            if k in DIRECT:
                for part in range(NC):
                    arrived(k, part)
            elif k == LEVELS:
                @pl.when(z == NZ - 1)
                def _():
                    for part in range(NC):
                        arrived(k, part)

                @pl.when(z < NZ - 1)
                def _():
                    arrived_whole(k)
            else:
                arrived_whole(k)
            if k == 2:
                @pl.when(z < NZ - 1)
                def _():
                    forward().start()
            if k == LEVELS + 1:
                backward().start()
            for delta in spread_to(k):
                if k <= LEVELS:
                    spread(k, delta, 0 if k in HALVED else None).start()
                else:
                    @pl.when(y + delta >= NY)
                    def _():
                        spread(k, delta).start()

    opposite = lax.rem(y + 2, NY)

    def chain(k):
        return remote(
            far.at[slot(k - 1, opposite)], far.at[slot(k, opposite)], x_ss.at[k], y_rs.at[k, 2], dev(z + 1, y, c)
        )

    def came(k, delta, half=None):
        ref, at = whole_or_half(slot(k, lax.rem(y + NY - delta, NY)), half), delta + NY * (half or 0)
        remote(ref, ref, y_ss.at[k, at], y_rs.at[k, at], d).wait_recv()

    def chain_on(k):
        if k not in CHAINED:
            return

        @pl.when(z >= k - 1)
        def _():
            came(k - 1, 2)

            @pl.when(z < NZ - 1)
            def _():
                chain(k).start()

    pass_on(1)

    wait_half(2)

    def cols(p):
        return pl.ds(pl.multiple_of(p * 128, 128), 128)

    def lanes(head, group):
        return slice(head * ROWS + group * 128, head * ROWS + (group + 1) * 128)

    first_rows = iota((128, 128), 0) < HEAD_DIM
    nothing = jnp.zeros((128, 128), jnp.bfloat16)
    for p in range(PAIRS):
        for group in range(2):
            part = qb[2 * group : 2 * group + 2, :, p * 128 : (p + 1) * 128].reshape(128, 128)
            turned = (part * jnp.bfloat16(HEAD_DIM ** -0.5)).T
            qm[p, :, lanes(0, group)] = jnp.where(first_rows, turned, nothing)
            qm[p, :, lanes(1, group)] = jnp.where(first_rows, nothing, turned)

    first_frame = iota((1, 128), 1) < TOK

    def own_frame(p, carry):
        def two_frames(ref, group):
            return ref[2 * group : 2 * group + 2, :, cols(p)].reshape(128, 128)

        keys = [two_frames(kb, group) for group in range(2)]
        values = [two_frames(vb, group) for group in range(2)]
        scores = []
        for head in range(2):
            for group in range(2):
                both = nn(keys[group], qm[p, :, lanes(head, group)])
                scores.append(jnp.where(first_frame, both[:TOK], both[TOK:]))
        scores = jnp.concatenate(scores, axis=1)
        top = jnp.max(scores, axis=0, keepdims=True)
        weights = jnp.exp(scores - top)
        tops[p] = top
        sums[p] = jnp.sum(weights, axis=0, keepdims=True)
        for head in range(2):
            for group in range(2):
                part = weights[:, lanes(head, group)]
                apart = jnp.concatenate(
                    [jnp.where(first_frame, part, 0.0), jnp.where(first_frame, 0.0, part)], axis=0
                ).astype(jnp.bfloat16)
                acc[p, :, lanes(head, group)] = tn(values[group], apart)[head * HEAD_DIM : (head + 1) * HEAD_DIM]
        return carry

    pass_on(2)
    pass_on(5)
    lax.fori_loop(0, 3, own_frame, 0, unroll=3)
    chain_on(2)
    pass_on(3)
    pass_on(4)
    for k in HALVED:
        @pl.when(z >= k)
        def _():
            for delta in spread_to(k):
                spread(k, delta, 1).start()
    lax.fori_loop(3, PAIRS, own_frame, 0, unroll=3)

    for k in range(1, LEVELS + 2):
        @pl.when(z >= k)
        def _():
            ref = clips.at[LEVELS + 1 - k]
            remote(ref, ref, cz_ss.at[k], cz_rs.at[k], d).wait_recv()
    table = clips[...].reshape(8, 128)
    own_first = BASE + 4 * y
    query_clip = [
        jnp.sum(jnp.where(lane == 4 * y + i, table[LEVELS + 1 : LEVELS + 2], 0.0), axis=1, keepdims=True)
        for i in range(FPC)
    ]
    table = table.astype(jnp.bfloat16)
    ones = jnp.ones((128, 128), jnp.bfloat16)

    def key_clips(numbers, rows):
        pick = (numbers // (NY * FPC))[:, :8] == iota((rows, 8), 1)
        level = jnp.dot(pick.astype(jnp.float32).astype(jnp.bfloat16), table, preferred_element_type=jnp.float32)
        one = jnp.where(lax.rem(numbers, NY * FPC) == iota((rows, 128), 1), level, 0.0)
        return jnp.dot(one.astype(jnp.bfloat16), ones, preferred_element_type=jnp.float32)

    def far_numbers(shape):
        n = iota(shape, 0)
        at, frame = n // BLK, lax.rem(n, BLK) // FAR
        step = at + NY - 1
        col = lax.rem(step, NY)
        level = functools.reduce(
            lambda found, k: jnp.where(step // NY == ORDER.index(k) + 1, k, found), ORDER, 0
        )
        regular = (LEVELS + 1 - level) * (NY * FPC) + col * FPC + frame
        shared = jnp.where(col < y, BASE, 0) + col * FPC + frame
        held = jnp.where((at >= MIXED) & (at < MIXED + NY), shared, regular)
        return jnp.where(at == OWN, own_first + frame, held)

    def near_numbers(shape):
        return own_first - 2 + iota(shape, 0) // NEAR_ROWS

    floor = (LEVELS + 1 - z) * (NY * FPC)
    for numbers, rows, bias in ((near_numbers, NKN, bias_near), (far_numbers, NKF, bias_far)):
        number = numbers((rows, 128))
        clip_of = key_clips(number, rows)
        for group in range(2):
            distance = own_first + 2 * group + lane // TOK - number
            seen = (distance >= 1) & (distance <= 2) if rows == NKN else distance > 2
            clip_here = jnp.where(first_frame, query_clip[2 * group], query_clip[2 * group + 1])
            ok = seen & (number >= floor) & (clip_of == clip_here)
            bias[:, group * 128 : (group + 1) * 128] = jnp.where(ok, 0.0, NEG)

    @pl.when(chip > 0)
    def _():
        ref = near.at[:, pl.ds(0, 2 * NEAR_ROWS)]
        remote(ref, ref, near_ss.at[0], near_rs.at[0], d).wait_recv()

    chain_on(3)

    def level_here(k, half=None):
        @pl.when(z >= k)
        def _():
            for delta in range(1, NY):
                if not (delta == 2 and k + 1 in CHAINED):
                    came(k, delta, half)

    def shared_here():
        for delta in range(1, NY):
            @pl.when(y >= delta)
            def _():
                for part in range(NC):
                    ref = far.at[MIXED + lax.rem(y + NY - delta, NY), part]
                    remote(ref, ref, m_ss.at[delta, 0], m_rs.at[delta, part], d).wait_recv()

            @pl.when((y < delta) & (z >= LEVELS + 1))
            def _():
                came(LEVELS + 1, delta)

    ref = far.at[OWN, 1 - c]
    remote(ref, ref, own_ss.at[0], own_rs.at[0], d).wait_recv()

    theirs = pl.ds(2 * (1 - c), 2)

    def out_local(p):
        return pltpu.make_async_copy(
            ob.at[p, mine], out_hbm.at[:, :, pl.ds(pl.multiple_of(lo + p * 128, 128), 128)], o_ls.at[p]
        )

    def out_remote(p):
        return remote(
            ob.at[p, theirs], out_hbm.at[:, :, pl.ds(pl.multiple_of(lo + p * 128, 128), 128)],
            o_ss.at[p], o_rs.at[p], sibling,
        )

    def far_rows(p, first, last):
        rows = (last - first) * BLK
        both = far[first:last, :, :, cols(p)].astype(jnp.float32).reshape(rows // 8, 2, 8, 128)
        return [both[:, n].reshape(rows, 128).astype(jnp.bfloat16) for n in range(2)]

    def join(p, keys, values, bias):
        scores = nn(keys, qm[p]) + jnp.concatenate([bias, bias], axis=1)
        old = tops[p]
        top = jnp.maximum(old, jnp.max(scores, axis=0, keepdims=True))
        factor = jnp.exp(old - top)
        weights = jnp.exp(scores - top)
        total = sums[p] * factor + jnp.sum(weights, axis=0, keepdims=True)
        weights = weights.astype(jnp.bfloat16)
        turned = values.T
        summed = [
            nn(turned[n * HEAD_DIM : (n + 1) * HEAD_DIM], weights[:, n * ROWS : (n + 1) * ROWS]) for n in range(2)
        ]
        return top, total, acc[p] * factor + jnp.concatenate(summed, axis=1)

    def keep(part):
        joined = [join(p, *part(p)) for p in range(PAIRS)]
        for p, (top, total, summed) in enumerate(joined):
            tops[p], sums[p], acc[p] = top, total, summed

    def nearest(p):
        keys, values = far_rows(p, 0, CHUNKS[0])
        keys = jnp.concatenate([near[0, :NKN, cols(p)], keys], axis=0)
        values = jnp.concatenate([near[1, :NKN, cols(p)], values], axis=0)
        return keys, values, jnp.concatenate([bias_near[...], bias_far[: CHUNKS[0] * BLK]], axis=0)

    def middle(p):
        return *far_rows(p, *CHUNKS), bias_far[CHUNKS[0] * BLK : CHUNKS[1] * BLK]

    def put(p, total, summed):
        result = (summed / total).astype(jnp.bfloat16)
        for group in range(2):
            turned = jnp.concatenate([result[:, lanes(head, group)] for head in range(2)], axis=0).T
            ob[p, 2 * group] = turned[:TOK]
            ob[p, 2 * group + 1] = turned[TOK:]

    level_here(1)
    keep(nearest)
    level_here(2)
    shared_here()
    keep(middle)
    def send_out(group):
        for p in group:
            out_remote(p).start()
            out_local(p).start()

    groups = (range(0, 3), range(3, PAIRS))

    @pl.when(z >= 3)
    def _():
        for half, group in enumerate(groups):
            for k in HALVED:
                level_here(k, half)
            for p in group:
                put(p, *join(p, *far_rows(p, CHUNKS[1], SLOTS), bias_far[CHUNKS[1] * BLK :])[1:])
            send_out(group)

    @pl.when(z < 3)
    def _():
        for group in groups:
            for p in group:
                put(p, sums[p], acc[p])
            send_out(group)

    for p in range(PAIRS):
        out_local(p).wait()
        out_remote(p).wait_send()
        ref = out_hbm.at[:, :, pl.ds(pl.multiple_of(hi + p * 128, 128), 128)]
        remote(ref, ref, o_ss.at[p], o_rs.at[p], sibling).wait_recv()
    for n in range(3):
        halves[n].wait_send()
    for cp in level_sends:
        cp.wait_send()
    across.wait_send()
    each_rise(lambda cp: cp.wait_send())
    each_mixed(lambda cp: cp.wait_send())

    @pl.when(z >= LEVELS + 1)
    def _():
        backward().wait_send()

    @pl.when((z >= 2) & (z < NZ - 1))
    def _():
        forward().wait_send()

    for k in CHAINED:
        @pl.when((z >= k - 1) & (z < NZ - 1))
        def _():
            chain(k).wait_send()

    for k in range(1, LEVELS + 2):
        @pl.when(z + k < NZ)
        def _():
            remote(clips.at[LEVELS + 1], clips.at[LEVELS + 1 - k], cz_ss.at[k], cz_rs.at[k], d).wait_send()

    @pl.when(chip < NZ * NY - 1)
    def _():
        near_out.wait_send()

    for k in ORDER:
        for delta in spread_to(k):
            @pl.when((z >= k) if k <= LEVELS else ((z >= k) & (y + delta >= NY)))
            def _():
                for half in (0, 1) if k in HALVED else (None,):
                    spread(k, delta, half).wait_send()


def on_device(queries, key_states, value_states, clip_ids):
    bf, f32 = jnp.bfloat16, jnp.float32
    dma = pltpu.SemaphoreType.DMA
    anywhere = pl.BlockSpec(memory_space=pltpu.HBM)
    return pl.pallas_call(
        kernel,
        out_shape=jax.ShapeDtypeStruct(queries.shape, bf),
        in_specs=[anywhere] * 4,
        out_specs=anywhere,
        scratch_shapes=[
            pltpu.SMEM((2,), jnp.int32),
            pltpu.VMEM((2, TOK, 2 * HALF), bf),
            pltpu.VMEM((2, TOK, 2 * HALF), bf),
            pltpu.VMEM((FPC, TOK, HALF), bf),
            pltpu.VMEM((FPC, TOK, HALF), bf),
            pltpu.VMEM((FPC, TOK, HALF), bf),
            pltpu.VMEM((2, BLK, HALF), bf),
            pltpu.VMEM((SLOTS, NC, BLK, HALF), bf),
            pltpu.VMEM((2, 6 * NEAR_ROWS, HALF), bf),
            pltpu.VMEM((PAIRS, 128, LANES), bf),
            pltpu.VMEM((NY * NC, 1, 128), f32),
            pltpu.VMEM((8, 1, 128), f32),
            pltpu.VMEM((NKF, ROWS), f32),
            pltpu.VMEM((NKN, ROWS), f32),
            pltpu.VMEM((PAIRS, HEAD_DIM, LANES), f32),
            pltpu.VMEM((PAIRS, 1, LANES), f32),
            pltpu.VMEM((PAIRS, 1, LANES), f32),
            pltpu.VMEM((PAIRS, FPC, TOK, 128), bf),
            dma((6,)),
            dma((3,)), dma((3,)),
            dma((1,)), dma((1,)),
            dma((LEVELS + 2, NC)), dma((LEVELS + 2, NC)),
            dma((NY, NC)), dma((NY, NC)),
            dma((LEVELS + 2, 2 * NY)), dma((LEVELS + 2, 2 * NY)), dma((LEVELS + 2,)),
            dma((1,)), dma((1,)),
            dma((NY * NC,)), dma((NY * NC,)),
            dma((LEVELS + 2,)), dma((LEVELS + 2,)),
            dma((PAIRS,)), dma((PAIRS,)), dma((PAIRS,)),
        ],
        compiler_params=pltpu.CompilerParams(
            collective_id=0, has_side_effects=True, vmem_limit_bytes=64 << 20
        ),
        cost_estimate=pl.CostEstimate(flops=1 << 30, bytes_accessed=4 << 20, transcendentals=1 << 21),
    )(queries, key_states, value_states, clip_ids)


def solution(mesh):
    frames = P(("dp", "tm"), None, None)
    return jax.shard_map(
        on_device,
        mesh=mesh,
        in_specs=(frames, frames, frames, P(("dp", "tm"))),
        out_specs=frames,
        check_vma=False,
    )
```

```python
import functools

import jax
import jax.numpy as jnp
from jax import lax
from jax.experimental import pallas as pl
from jax.experimental.pallas import tpu as pltpu
from jax.sharding import PartitionSpec as P

HEAD_DIM = 64
SIDE = 8
TOK = 64
NZ, NY, NC = 8, 4, 2
FPC = 4
HALF = 768
PAIRS = HALF // 128
ROWS = FPC * TOK
LANES = 2 * ROWS
FAR = 4
BLK = FPC * FAR
LEVELS = 4
OWN = 0
ORDER = (1, 2, 5, 3, 4)
FIRST = {k: 1 + n * NY for n, k in enumerate(ORDER)}
DIRECT = (1, 2, 5)
LEAP = 3
HALVED = (3, 4)
CHAINED = (2,)
MIXED = FIRST[LEVELS + 1]
SLOTS = 1 + 5 * NY
CHUNKS = (FIRST[2], FIRST[3])
NKF = SLOTS * BLK
NEAR_ROWS = 16
NKN = 5 * NEAR_ROWS
FLAT = (LEVELS + 2) * NY * FPC
BASE = FLAT - NY * FPC
NEG = -1e30
MESH = pl.DeviceIdType.MESH


def iota(shape, dim):
    return lax.broadcasted_iota(jnp.int32, shape, dim)


def remote(src, dst, ss, rs, to):
    return pltpu.make_async_remote_copy(
        src_ref=src, dst_ref=dst, send_sem=ss, recv_sem=rs, device_id={"tm": to}, device_id_type=MESH
    )


def nt(a, b):
    return lax.dot_general(a, b, (((1,), (1,)), ((), ())), preferred_element_type=jnp.float32)


def nn(a, b):
    return jnp.dot(a, b, preferred_element_type=jnp.float32)


def tn(a, b):
    return lax.dot_general(a, b, (((0,), (0,)), ((), ())), preferred_element_type=jnp.float32)


def kernel(
    q_hbm, k_hbm, v_hbm, clip_hbm, out_hbm,
    clip_ref, kf, vf, qb, kb, vb, pooled, far, near, qm, level_clips, clips, bias_far, bias_near, acc, tops, sums, ob,
    in_sem, sib_ss, sib_rs, own_ss, own_rs, z_ss, z_rs, m_ss, m_rs, y_ss, y_rs, x_ss,
    near_ss, near_rs, cy_ss, cy_rs, cz_ss, cz_rs, o_ss, o_rs, o_ls,
):
    d = lax.axis_index("tm")
    z, y, c = d // (NY * NC), lax.rem(d // NC, NY), lax.rem(d, NC)
    chip = d // NC

    def dev(zz, yy, cc):
        return zz * (NY * NC) + yy * NC + cc

    sibling = dev(z, y, 1 - c)

    barrier = pltpu.get_barrier_semaphore()

    def greet(to):
        pl.semaphore_signal(barrier, inc=1, device_id={"tm": to}, device_id_type=MESH)

    for k in DIRECT[::-1]:
        @pl.when(z >= k)
        def _():
            for core in range(NC):
                greet(dev(z - k, y, core))

    @pl.when((y == 0) & (z > 0))
    def _():
        greet(dev(z - 1, NY - 1, c))

    for yy in range(1, NY):
        for cc in range(NC):
            greet(dev(z, lax.rem(y + yy, NY), cc))
    greet(sibling)

    lo = pl.multiple_of(c * HALF, 128)
    hi = pl.multiple_of((1 - c) * HALF, 128)
    mine = pl.ds(2 * c, 2)
    whole = []
    for n, (src, dst) in enumerate(((k_hbm, kf), (v_hbm, vf))):
        cp = pltpu.make_async_copy(src, dst, in_sem.at[n])
        cp.start()
        whole.append(cp)
    clip_copy = pltpu.make_async_copy(clip_hbm, clip_ref, in_sem.at[2])
    clip_copy.start()
    local = []
    for n, (src, dst) in enumerate(((k_hbm, kb), (v_hbm, vb), (q_hbm, qb))):
        cp = pltpu.make_async_copy(src.at[:, :, pl.ds(lo, HALF)], dst.at[mine], in_sem.at[3 + n])
        cp.start()
        local.append(cp)

    for k in ORDER:
        for col in range(NY):
            @pl.when((z < k) & (col >= y) if k == LEVELS + 1 else z < k)
            def _():
                far[FIRST[k] + col] = jnp.zeros(far.shape[1:], far.dtype)

    @pl.when(chip == 0)
    def _():
        near[:, : 2 * NEAR_ROWS] = jnp.zeros((2, 2 * NEAR_ROWS, HALF), jnp.bfloat16)

    for k in range(1, LEVELS + 2):
        @pl.when(z < (3 if k == LEVELS else k))
        def _():
            clips[LEVELS + 1 - k] = jnp.zeros((1, 128), jnp.float32)
    for n in range(LEVELS + 2, 8):
        clips[n] = jnp.zeros((1, 128), jnp.float32)

    def pool_matrix(rows, frames, side):
        r, t = iota((rows, frames * TOK), 0), iota((rows, frames * TOK), 1)
        frame, token = t // TOK, lax.rem(t, TOK)
        cells = SIDE // side
        at = frame * cells * cells + (token // SIDE // side) * cells + lax.rem(token, SIDE) // side
        return jnp.where(r == at, 1.0 / (side * side), 0.0).astype(jnp.bfloat16)

    far_pool = pool_matrix(2 * FAR, 2, 4)
    means = []
    for n, full in enumerate((kf, vf)):
        whole[n].wait()
        means.append(nn(far_pool, full[...].reshape(2 * TOK, 2 * HALF)))
    means = jnp.concatenate(means, axis=0).astype(jnp.bfloat16)
    for n in range(2):
        pooled[n] = means[:, n * HALF : (n + 1) * HALF]

    up = sum(jnp.where(z + k < NZ, NC, 0) for k in DIRECT)
    next_near = jnp.where((y == NY - 1) & (z < NZ - 1), 1, 0)
    pl.semaphore_wait(barrier, (NY - 1) * NC + 1 + up + next_near)

    def slot(k, col):
        return FIRST[k] + col

    def rise(k, core):
        return remote(
            pooled.at[core], far.at[slot(k, y), c], z_ss.at[k, core], z_rs.at[k, c], dev(z + k, y, core)
        )

    def mixed(delta, core):
        return remote(
            pooled.at[core], far.at[MIXED + y, c], m_ss.at[delta, core], m_rs.at[delta, c],
            dev(z, lax.rem(y + delta, NY), core),
        )

    def each_rise(act):
        for k in (1, 5, 2):
            @pl.when(z + k < NZ)
            def _():
                for core in range(NC):
                    act(rise(k, core))

    def each_mixed(act):
        for delta in (1, 3, 2):
            @pl.when(y + delta < NY)
            def _():
                for core in range(NC):
                    act(mixed(delta, core))

    each_rise(lambda cp: cp.start())
    each_mixed(lambda cp: cp.start())
    across = remote(pooled.at[1 - c], far.at[OWN, c], own_ss.at[0], own_rs.at[0], sibling)
    across.start()
    far[OWN, c] = pooled[c]

    halves = []
    for n, (src, dst) in enumerate(((k_hbm, kb), (v_hbm, vb), (q_hbm, qb))):
        cp = remote(src.at[:, :, pl.ds(hi, HALF)], dst.at[mine], sib_ss.at[n], sib_rs.at[n], sibling)
        cp.start()
        halves.append(cp)

    def wait_half(n):
        local[n].wait()
        other = (kb, vb, qb)[n].at[pl.ds(2 * (1 - c), 2)]
        remote(other, other, sib_ss.at[n], sib_rs.at[n], sibling).wait_recv()

    clip_copy.wait()
    row = y * NC + c
    lane = iota((1, 128), 1)
    level_clips[row] = sum(
        jnp.where(lane == 2 * row + n, clip_ref[n].astype(jnp.float32), 0.0) for n in range(2)
    )
    level_sends = []
    for n in range(1, NY * NC):
        to = lax.rem(row + n, NY * NC)
        ref = level_clips.at[row]
        cp = remote(ref, ref, cy_ss.at[n], cy_rs.at[n], z * (NY * NC) + to)
        cp.start()
        level_sends.append(cp)

    near_pool = pool_matrix(NEAR_ROWS * FPC, FPC, 2)
    for n, full in enumerate((kb, vb)):
        wait_half(n)
        near[n, 2 * NEAR_ROWS :] = nn(near_pool, full[...].reshape(ROWS, HALF)).astype(jnp.bfloat16)

    near_out = remote(
        near.at[:, pl.ds(4 * NEAR_ROWS, 2 * NEAR_ROWS)], near.at[:, pl.ds(0, 2 * NEAR_ROWS)],
        near_ss.at[0], near_rs.at[0], jnp.minimum((chip + 1) * NC + c, NZ * NY * NC - 1),
    )

    @pl.when(chip < NZ * NY - 1)
    def _():
        near_out.start()

    for n in range(1, NY * NC):
        ref = level_clips.at[lax.rem(row + NY * NC - n, NY * NC)]
        remote(ref, ref, cy_ss.at[n], cy_rs.at[n], d).wait_recv()
    clips[LEVELS + 1] = jnp.sum(level_clips[...], axis=0)
    def clips_up(k):
        return remote(
            clips.at[LEVELS + 1], clips.at[LEVELS + 1 - k], cz_ss.at[k], cz_rs.at[k], dev(z + k, y, c)
        )

    def clips_on():
        return remote(clips.at[3:5], clips.at[1:3], cz_ss.at[3], cz_rs.at[3], dev(z + 2, y, c))

    def clips_came(k):
        ref = clips.at[1:3] if k == 3 else clips.at[LEVELS + 1 - k]
        remote(ref, ref, cz_ss.at[k], cz_rs.at[k], d).wait_recv()

    for k in DIRECT:
        @pl.when(z + k < NZ)
        def _():
            clips_up(k).start()

    def spread(k, delta, half=None):
        ref, at = whole_or_half(slot(k, y), half), delta + NY * (half or 0)
        return remote(ref, ref, y_ss.at[k, at], y_rs.at[k, at], dev(z, lax.rem(y + delta, NY), c))

    def whole_or_half(at, half):
        if half is None:
            return far.at[at]
        return far.at[at, :, :, half * (HALF // 2) : (half + 1) * (HALF // 2)]

    def arrived(k, part):
        ref = far.at[slot(k, y), part]
        remote(ref, ref, z_ss.at[k, 0], z_rs.at[k, part], d).wait_recv()

    def arrived_whole(k):
        ref = far.at[slot(k, y)]
        remote(ref, ref, z_ss.at[k, 0], z_rs.at[k, 0], d).wait_recv()

    def forward():
        return remote(far.at[slot(2, y)], far.at[slot(3, y)], z_ss.at[3, 0], z_rs.at[3, 0], dev(z + 1, y, c))

    def leap():
        return remote(
            far.at[slot(2, y)], far.at[slot(4, y)], z_ss.at[4, 1], z_rs.at[4, 0], dev(jnp.minimum(z + 2, NZ - 1), y, c)
        )

    def backward():
        return remote(far.at[slot(5, y)], far.at[slot(4, y)], z_ss.at[4, 0], z_rs.at[4, 0], dev(z - 1, y, c))

    def spread_to(k):
        return (1, 3) if k in CHAINED else (2, 1, 3)

    def pass_on(k):
        @pl.when(z >= k)
        def _():
            if k in DIRECT:
                for part in range(NC):
                    arrived(k, part)
            else:
                arrived_whole(k)
            if k == 2:
                @pl.when(z < NZ - 1)
                def _():
                    forward().start()

                @pl.when((z >= LEAP) & (z <= NZ - 3))
                def _():
                    leap().start()
            if k == LEVELS + 1:
                @pl.when(z < LEAP + 3)
                def _():
                    backward().start()
            for delta in spread_to(k):
                if k <= LEVELS:
                    spread(k, delta, 0 if k in HALVED else None).start()
                else:
                    @pl.when(y + delta >= NY)
                    def _():
                        spread(k, delta).start()

    opposite = lax.rem(y + 2, NY)

    def chain(k):
        return remote(
            far.at[slot(k - 1, opposite)], far.at[slot(k, opposite)], x_ss.at[k], y_rs.at[k, 2], dev(z + 1, y, c)
        )

    def came(k, delta, half=None):
        ref, at = whole_or_half(slot(k, lax.rem(y + NY - delta, NY)), half), delta + NY * (half or 0)
        remote(ref, ref, y_ss.at[k, at], y_rs.at[k, at], d).wait_recv()

    def chain_on(k):
        if k not in CHAINED:
            return

        @pl.when(z >= k - 1)
        def _():
            came(k - 1, 2)

            @pl.when(z < NZ - 1)
            def _():
                chain(k).start()

    pass_on(1)

    wait_half(2)

    def cols(p):
        return pl.ds(pl.multiple_of(p * 128, 128), 128)

    def lanes(head, group):
        return slice(head * ROWS + group * 128, head * ROWS + (group + 1) * 128)

    first_rows = iota((128, 128), 0) < HEAD_DIM
    nothing = jnp.zeros((128, 128), jnp.bfloat16)
    for p in range(PAIRS):
        for group in range(2):
            part = qb[2 * group : 2 * group + 2, :, p * 128 : (p + 1) * 128].reshape(128, 128)
            turned = (part * jnp.bfloat16(HEAD_DIM ** -0.5)).T
            qm[p, :, lanes(0, group)] = jnp.where(first_rows, turned, nothing)
            qm[p, :, lanes(1, group)] = jnp.where(first_rows, nothing, turned)

    first_frame = iota((1, 128), 1) < TOK

    def own_frame(p, carry):
        def two_frames(ref, group):
            return ref[2 * group : 2 * group + 2, :, cols(p)].reshape(128, 128)

        keys = [two_frames(kb, group) for group in range(2)]
        values = [two_frames(vb, group) for group in range(2)]
        scores = []
        for head in range(2):
            for group in range(2):
                both = nn(keys[group], qm[p, :, lanes(head, group)])
                scores.append(jnp.where(first_frame, both[:TOK], both[TOK:]))
        scores = jnp.concatenate(scores, axis=1)
        top = jnp.max(scores, axis=0, keepdims=True)
        weights = jnp.exp(scores - top)
        tops[p] = top
        sums[p] = jnp.sum(weights, axis=0, keepdims=True)
        for head in range(2):
            for group in range(2):
                part = weights[:, lanes(head, group)]
                apart = jnp.concatenate(
                    [jnp.where(first_frame, part, 0.0), jnp.where(first_frame, 0.0, part)], axis=0
                ).astype(jnp.bfloat16)
                acc[p, :, lanes(head, group)] = tn(values[group], apart)[head * HEAD_DIM : (head + 1) * HEAD_DIM]
        return carry

    pass_on(2)
    pass_on(5)
    for k in (1, 2):
        @pl.when(z >= k)
        def _():
            clips_came(k)

    @pl.when((z >= 1) & (z < NZ - 2))
    def _():
        clips_on().start()

    lax.fori_loop(0, 3, own_frame, 0, unroll=3)
    chain_on(2)
    pass_on(3)
    pass_on(4)
    for k in HALVED:
        @pl.when(z >= k)
        def _():
            for delta in spread_to(k):
                spread(k, delta, 1).start()
    lax.fori_loop(3, PAIRS, own_frame, 0, unroll=3)

    for k in (3, LEVELS + 1):
        @pl.when(z >= k)
        def _():
            clips_came(k)
    table = clips[...].reshape(8, 128)
    own_first = BASE + 4 * y
    query_clip = [
        jnp.sum(jnp.where(lane == 4 * y + i, table[LEVELS + 1 : LEVELS + 2], 0.0), axis=1, keepdims=True)
        for i in range(FPC)
    ]
    table = table.astype(jnp.bfloat16)
    ones = jnp.ones((128, 128), jnp.bfloat16)

    def key_clips(numbers, rows):
        pick = (numbers // (NY * FPC))[:, :8] == iota((rows, 8), 1)
        level = jnp.dot(pick.astype(jnp.float32).astype(jnp.bfloat16), table, preferred_element_type=jnp.float32)
        one = jnp.where(lax.rem(numbers, NY * FPC) == iota((rows, 128), 1), level, 0.0)
        return jnp.dot(one.astype(jnp.bfloat16), ones, preferred_element_type=jnp.float32)

    def far_numbers(shape):
        n = iota(shape, 0)
        at, frame = n // BLK, lax.rem(n, BLK) // FAR
        step = at + NY - 1
        col = lax.rem(step, NY)
        level = functools.reduce(
            lambda found, k: jnp.where(step // NY == ORDER.index(k) + 1, k, found), ORDER, 0
        )
        regular = (LEVELS + 1 - level) * (NY * FPC) + col * FPC + frame
        shared = jnp.where(col < y, BASE, 0) + col * FPC + frame
        held = jnp.where((at >= MIXED) & (at < MIXED + NY), shared, regular)
        return jnp.where(at == OWN, own_first + frame, held)

    def near_numbers(shape):
        return own_first - 2 + iota(shape, 0) // NEAR_ROWS

    floor = (LEVELS + 1 - z) * (NY * FPC)
    for numbers, rows, bias in ((near_numbers, NKN, bias_near), (far_numbers, NKF, bias_far)):
        number = numbers((rows, 128))
        clip_of = key_clips(number, rows)
        for group in range(2):
            distance = own_first + 2 * group + lane // TOK - number
            seen = (distance >= 1) & (distance <= 2) if rows == NKN else distance > 2
            clip_here = jnp.where(first_frame, query_clip[2 * group], query_clip[2 * group + 1])
            ok = seen & (number >= floor) & (clip_of == clip_here)
            bias[:, group * 128 : (group + 1) * 128] = jnp.where(ok, 0.0, NEG)

    @pl.when(chip > 0)
    def _():
        ref = near.at[:, pl.ds(0, 2 * NEAR_ROWS)]
        remote(ref, ref, near_ss.at[0], near_rs.at[0], d).wait_recv()

    chain_on(3)

    def level_here(k, half=None):
        @pl.when(z >= k)
        def _():
            for delta in range(1, NY):
                if not (delta == 2 and k + 1 in CHAINED):
                    came(k, delta, half)

    def shared_here():
        for delta in range(1, NY):
            @pl.when(y >= delta)
            def _():
                for part in range(NC):
                    ref = far.at[MIXED + lax.rem(y + NY - delta, NY), part]
                    remote(ref, ref, m_ss.at[delta, 0], m_rs.at[delta, part], d).wait_recv()

            @pl.when((y < delta) & (z >= LEVELS + 1))
            def _():
                came(LEVELS + 1, delta)

    ref = far.at[OWN, 1 - c]
    remote(ref, ref, own_ss.at[0], own_rs.at[0], d).wait_recv()

    theirs = pl.ds(2 * (1 - c), 2)

    def out_local(p):
        return pltpu.make_async_copy(
            ob.at[p, mine], out_hbm.at[:, :, pl.ds(pl.multiple_of(lo + p * 128, 128), 128)], o_ls.at[p]
        )

    def out_remote(p):
        return remote(
            ob.at[p, theirs], out_hbm.at[:, :, pl.ds(pl.multiple_of(lo + p * 128, 128), 128)],
            o_ss.at[p], o_rs.at[p], sibling,
        )

    def far_rows(p, first, last):
        rows = (last - first) * BLK
        both = far[first:last, :, :, cols(p)].astype(jnp.float32).reshape(rows // 8, 2, 8, 128)
        return [both[:, n].reshape(rows, 128).astype(jnp.bfloat16) for n in range(2)]

    def join(p, keys, values, bias):
        scores = nn(keys, qm[p]) + jnp.concatenate([bias, bias], axis=1)
        old = tops[p]
        top = jnp.maximum(old, jnp.max(scores, axis=0, keepdims=True))
        factor = jnp.exp(old - top)
        weights = jnp.exp(scores - top)
        total = sums[p] * factor + jnp.sum(weights, axis=0, keepdims=True)
        weights = weights.astype(jnp.bfloat16)
        turned = values.T
        summed = [
            nn(turned[n * HEAD_DIM : (n + 1) * HEAD_DIM], weights[:, n * ROWS : (n + 1) * ROWS]) for n in range(2)
        ]
        return top, total, acc[p] * factor + jnp.concatenate(summed, axis=1)

    def keep(part):
        joined = [join(p, *part(p)) for p in range(PAIRS)]
        for p, (top, total, summed) in enumerate(joined):
            tops[p], sums[p], acc[p] = top, total, summed

    def nearest(p):
        keys, values = far_rows(p, 0, CHUNKS[0])
        keys = jnp.concatenate([near[0, :NKN, cols(p)], keys], axis=0)
        values = jnp.concatenate([near[1, :NKN, cols(p)], values], axis=0)
        return keys, values, jnp.concatenate([bias_near[...], bias_far[: CHUNKS[0] * BLK]], axis=0)

    def middle(p):
        return *far_rows(p, *CHUNKS), bias_far[CHUNKS[0] * BLK : CHUNKS[1] * BLK]

    def put(p, total, summed):
        result = (summed / total).astype(jnp.bfloat16)
        for group in range(2):
            turned = jnp.concatenate([result[:, lanes(head, group)] for head in range(2)], axis=0).T
            ob[p, 2 * group] = turned[:TOK]
            ob[p, 2 * group + 1] = turned[TOK:]

    level_here(1)
    keep(nearest)
    level_here(2)
    shared_here()
    keep(middle)
    def send_out(group):
        for p in group:
            out_remote(p).start()
            out_local(p).start()

    groups = (range(0, 3), range(3, PAIRS))

    @pl.when(z >= 3)
    def _():
        for half, group in enumerate(groups):
            for k in HALVED:
                level_here(k, half)
            for p in group:
                put(p, *join(p, *far_rows(p, CHUNKS[1], SLOTS), bias_far[CHUNKS[1] * BLK :])[1:])
            send_out(group)

    @pl.when(z < 3)
    def _():
        for group in groups:
            for p in group:
                put(p, sums[p], acc[p])
            send_out(group)

    for p in range(PAIRS):
        out_local(p).wait()
        out_remote(p).wait_send()
        ref = out_hbm.at[:, :, pl.ds(pl.multiple_of(hi + p * 128, 128), 128)]
        remote(ref, ref, o_ss.at[p], o_rs.at[p], sibling).wait_recv()
    for n in range(3):
        halves[n].wait_send()
    for cp in level_sends:
        cp.wait_send()
    across.wait_send()
    each_rise(lambda cp: cp.wait_send())
    each_mixed(lambda cp: cp.wait_send())

    @pl.when((z >= LEVELS + 1) & (z < LEAP + 3))
    def _():
        backward().wait_send()

    @pl.when((z >= 2) & (z < NZ - 1))
    def _():
        forward().wait_send()

    for k in CHAINED:
        @pl.when((z >= k - 1) & (z < NZ - 1))
        def _():
            chain(k).wait_send()

    for k in DIRECT:
        @pl.when(z + k < NZ)
        def _():
            clips_up(k).wait_send()

    @pl.when((z >= 1) & (z < NZ - 2))
    def _():
        clips_on().wait_send()

    @pl.when((z >= LEAP) & (z <= NZ - 3))
    def _():
        leap().wait_send()

    @pl.when(chip < NZ * NY - 1)
    def _():
        near_out.wait_send()

    for k in ORDER:
        for delta in spread_to(k):
            @pl.when((z >= k) if k <= LEVELS else ((z >= k) & (y + delta >= NY)))
            def _():
                for half in (0, 1) if k in HALVED else (None,):
                    spread(k, delta, half).wait_send()


def on_device(queries, key_states, value_states, clip_ids):
    bf, f32 = jnp.bfloat16, jnp.float32
    dma = pltpu.SemaphoreType.DMA
    anywhere = pl.BlockSpec(memory_space=pltpu.HBM)
    return pl.pallas_call(
        kernel,
        out_shape=jax.ShapeDtypeStruct(queries.shape, bf),
        in_specs=[anywhere] * 4,
        out_specs=anywhere,
        scratch_shapes=[
            pltpu.SMEM((2,), jnp.int32),
            pltpu.VMEM((2, TOK, 2 * HALF), bf),
            pltpu.VMEM((2, TOK, 2 * HALF), bf),
            pltpu.VMEM((FPC, TOK, HALF), bf),
            pltpu.VMEM((FPC, TOK, HALF), bf),
            pltpu.VMEM((FPC, TOK, HALF), bf),
            pltpu.VMEM((2, BLK, HALF), bf),
            pltpu.VMEM((SLOTS, NC, BLK, HALF), bf),
            pltpu.VMEM((2, 6 * NEAR_ROWS, HALF), bf),
            pltpu.VMEM((PAIRS, 128, LANES), bf),
            pltpu.VMEM((NY * NC, 1, 128), f32),
            pltpu.VMEM((8, 1, 128), f32),
            pltpu.VMEM((NKF, ROWS), f32),
            pltpu.VMEM((NKN, ROWS), f32),
            pltpu.VMEM((PAIRS, HEAD_DIM, LANES), f32),
            pltpu.VMEM((PAIRS, 1, LANES), f32),
            pltpu.VMEM((PAIRS, 1, LANES), f32),
            pltpu.VMEM((PAIRS, FPC, TOK, 128), bf),
            dma((6,)),
            dma((3,)), dma((3,)),
            dma((1,)), dma((1,)),
            dma((LEVELS + 2, NC)), dma((LEVELS + 2, NC)),
            dma((NY, NC)), dma((NY, NC)),
            dma((LEVELS + 2, 2 * NY)), dma((LEVELS + 2, 2 * NY)), dma((LEVELS + 2,)),
            dma((1,)), dma((1,)),
            dma((NY * NC,)), dma((NY * NC,)),
            dma((LEVELS + 2,)), dma((LEVELS + 2,)),
            dma((PAIRS,)), dma((PAIRS,)), dma((PAIRS,)),
        ],
        compiler_params=pltpu.CompilerParams(
            collective_id=0, has_side_effects=True, vmem_limit_bytes=64 << 20
        ),
        cost_estimate=pl.CostEstimate(flops=1 << 30, bytes_accessed=4 << 20, transcendentals=1 << 21),
    )(queries, key_states, value_states, clip_ids)


def solution(mesh):
    frames = P(("dp", "tm"), None, None)
    return jax.shard_map(
        on_device,
        mesh=mesh,
        in_specs=(frames, frames, frames, P(("dp", "tm"))),
        out_specs=frames,
        check_vma=False,
    )
```

```python
import functools

import jax
import jax.numpy as jnp
from jax import lax
from jax.experimental import pallas as pl
from jax.experimental.pallas import tpu as pltpu
from jax.sharding import PartitionSpec as P

HEAD_DIM = 64
SIDE = 8
TOK = 64
NZ, NY, NC = 8, 4, 2
FPC = 4
HALF = 768
PAIRS = HALF // 128
ROWS = FPC * TOK
LANES = 2 * ROWS
FAR = 4
BLK = FPC * FAR
LEVELS = 4
OWN = 0
ORDER = (1, 2, 5, 3, 4)
FIRST = {k: 1 + n * NY for n, k in enumerate(ORDER)}
DIRECT = (1, 2, 5)
LEAP = 3
HALVED = (3, 4)
CHAINED = (2,)
MIXED = FIRST[LEVELS + 1]
SLOTS = 1 + 5 * NY
CHUNKS = (FIRST[2], FIRST[3])
NKF = SLOTS * BLK
NEAR_ROWS = 16
NKN = 5 * NEAR_ROWS
FLAT = (LEVELS + 2) * NY * FPC
BASE = FLAT - NY * FPC
NEG = -1e30
MESH = pl.DeviceIdType.MESH


def iota(shape, dim):
    return lax.broadcasted_iota(jnp.int32, shape, dim)


def remote(src, dst, ss, rs, to):
    return pltpu.make_async_remote_copy(
        src_ref=src, dst_ref=dst, send_sem=ss, recv_sem=rs, device_id={"tm": to}, device_id_type=MESH
    )


def nt(a, b):
    return lax.dot_general(a, b, (((1,), (1,)), ((), ())), preferred_element_type=jnp.float32)


def nn(a, b):
    return jnp.dot(a, b, preferred_element_type=jnp.float32)


def tn(a, b):
    return lax.dot_general(a, b, (((0,), (0,)), ((), ())), preferred_element_type=jnp.float32)


def kernel(
    q_hbm, k_hbm, v_hbm, clip_hbm, out_hbm,
    clip_ref, kf, vf, qb, kb, vb, pooled, far, near, qm, level_clips, clips, bias_far, bias_near, acc, tops, sums, ob,
    in_sem, sib_ss, sib_rs, own_ss, own_rs, z_ss, z_rs, m_ss, m_rs, y_ss, y_rs, x_ss,
    near_ss, near_rs, cy_ss, cy_rs, cz_ss, cz_rs, o_ss, o_rs, o_ls,
):
    d = lax.axis_index("tm")
    z, y, c = d // (NY * NC), lax.rem(d // NC, NY), lax.rem(d, NC)
    chip = d // NC

    def dev(zz, yy, cc):
        return zz * (NY * NC) + yy * NC + cc

    sibling = dev(z, y, 1 - c)

    barrier = pltpu.get_barrier_semaphore()

    def greet(to):
        pl.semaphore_signal(barrier, inc=1, device_id={"tm": to}, device_id_type=MESH)

    for k in DIRECT[::-1]:
        @pl.when(z >= k)
        def _():
            for core in range(NC):
                greet(dev(z - k, y, core))

    @pl.when((y == 0) & (z > 0))
    def _():
        greet(dev(z - 1, NY - 1, c))

    for yy in range(1, NY):
        for cc in range(NC):
            greet(dev(z, lax.rem(y + yy, NY), cc))
    greet(sibling)

    lo = pl.multiple_of(c * HALF, 128)
    hi = pl.multiple_of((1 - c) * HALF, 128)
    mine = pl.ds(2 * c, 2)
    whole = []
    for n, (src, dst) in enumerate(((k_hbm, kf), (v_hbm, vf))):
        cp = pltpu.make_async_copy(src, dst, in_sem.at[n])
        cp.start()
        whole.append(cp)
    clip_copy = pltpu.make_async_copy(clip_hbm, clip_ref, in_sem.at[2])
    clip_copy.start()
    local = []
    for n, (src, dst) in enumerate(((k_hbm, kb), (v_hbm, vb), (q_hbm, qb))):
        cp = pltpu.make_async_copy(src.at[:, :, pl.ds(lo, HALF)], dst.at[mine], in_sem.at[3 + n])
        cp.start()
        local.append(cp)

    for k in ORDER:
        for col in range(NY):
            @pl.when((z < k) & (col >= y) if k == LEVELS + 1 else z < k)
            def _():
                far[FIRST[k] + col] = jnp.zeros(far.shape[1:], far.dtype)

    @pl.when(chip == 0)
    def _():
        near[:, : 2 * NEAR_ROWS] = jnp.zeros((2, 2 * NEAR_ROWS, HALF), jnp.bfloat16)

    for k in range(1, LEVELS + 2):
        @pl.when(z < (3 if k == LEVELS else k))
        def _():
            clips[LEVELS + 1 - k] = jnp.zeros((1, 128), jnp.float32)
    for n in range(LEVELS + 2, 8):
        clips[n] = jnp.zeros((1, 128), jnp.float32)

    def pool_matrix(rows, frames, side):
        r, t = iota((rows, frames * TOK), 0), iota((rows, frames * TOK), 1)
        frame, token = t // TOK, lax.rem(t, TOK)
        cells = SIDE // side
        at = frame * cells * cells + (token // SIDE // side) * cells + lax.rem(token, SIDE) // side
        return jnp.where(r == at, 1.0 / (side * side), 0.0).astype(jnp.bfloat16)

    far_pool = pool_matrix(2 * FAR, 2, 4)
    means = []
    for n, full in enumerate((kf, vf)):
        whole[n].wait()
        means.append(nn(far_pool, full[...].reshape(2 * TOK, 2 * HALF)))
    means = jnp.concatenate(means, axis=0).astype(jnp.bfloat16)
    for n in range(2):
        pooled[n] = means[:, n * HALF : (n + 1) * HALF]

    up = sum(jnp.where(z + k < NZ, NC, 0) for k in DIRECT)
    next_near = jnp.where((y == NY - 1) & (z < NZ - 1), 1, 0)
    pl.semaphore_wait(barrier, (NY - 1) * NC + 1 + up + next_near)

    def slot(k, col):
        return FIRST[k] + col

    def rise(k, core):
        return remote(
            pooled.at[core], far.at[slot(k, y), c], z_ss.at[k, core], z_rs.at[k, c], dev(z + k, y, core)
        )

    def mixed(delta, core):
        return remote(
            pooled.at[core], far.at[MIXED + y, c], m_ss.at[delta, core], m_rs.at[delta, c],
            dev(z, lax.rem(y + delta, NY), core),
        )

    def each_rise(act):
        for k in (1, 5, 2):
            @pl.when(z + k < NZ)
            def _():
                for core in range(NC):
                    act(rise(k, core))

    def each_mixed(act):
        for delta in (1, 3, 2):
            @pl.when(y + delta < NY)
            def _():
                for core in range(NC):
                    act(mixed(delta, core))

    halves = []
    for n, (src, dst) in enumerate(((k_hbm, kb), (v_hbm, vb), (q_hbm, qb))):
        cp = remote(src.at[:, :, pl.ds(hi, HALF)], dst.at[mine], sib_ss.at[n], sib_rs.at[n], sibling)
        cp.start()
        halves.append(cp)
    each_rise(lambda cp: cp.start())
    each_mixed(lambda cp: cp.start())
    across = remote(pooled.at[1 - c], far.at[OWN, c], own_ss.at[0], own_rs.at[0], sibling)
    across.start()
    far[OWN, c] = pooled[c]

    def wait_half(n):
        local[n].wait()
        other = (kb, vb, qb)[n].at[pl.ds(2 * (1 - c), 2)]
        remote(other, other, sib_ss.at[n], sib_rs.at[n], sibling).wait_recv()

    clip_copy.wait()
    row = y * NC + c
    lane = iota((1, 128), 1)
    level_clips[row] = sum(
        jnp.where(lane == 2 * row + n, clip_ref[n].astype(jnp.float32), 0.0) for n in range(2)
    )
    level_sends = []
    for n in range(1, NY * NC):
        to = lax.rem(row + n, NY * NC)
        ref = level_clips.at[row]
        cp = remote(ref, ref, cy_ss.at[n], cy_rs.at[n], z * (NY * NC) + to)
        cp.start()
        level_sends.append(cp)

    def near_out(n):
        return remote(
            near.at[n, pl.ds(4 * NEAR_ROWS, 2 * NEAR_ROWS)], near.at[n, pl.ds(0, 2 * NEAR_ROWS)],
            near_ss.at[n], near_rs.at[n], jnp.minimum((chip + 1) * NC + c, NZ * NY * NC - 1),
        )

    near_pool = pool_matrix(NEAR_ROWS * FPC, FPC, 2)
    for n, full in enumerate((kb, vb)):
        wait_half(n)
        near[n, 2 * NEAR_ROWS :] = nn(near_pool, full[...].reshape(ROWS, HALF)).astype(jnp.bfloat16)

        @pl.when(chip < NZ * NY - 1)
        def _():
            near_out(n).start()

    for n in range(1, NY * NC):
        ref = level_clips.at[lax.rem(row + NY * NC - n, NY * NC)]
        remote(ref, ref, cy_ss.at[n], cy_rs.at[n], d).wait_recv()
    clips[LEVELS + 1] = jnp.sum(level_clips[...], axis=0)
    def clips_up(k):
        return remote(
            clips.at[LEVELS + 1], clips.at[LEVELS + 1 - k], cz_ss.at[k], cz_rs.at[k], dev(z + k, y, c)
        )

    def clips_on():
        return remote(clips.at[3:5], clips.at[1:3], cz_ss.at[3], cz_rs.at[3], dev(z + 2, y, c))

    def clips_came(k):
        ref = clips.at[1:3] if k == 3 else clips.at[LEVELS + 1 - k]
        remote(ref, ref, cz_ss.at[k], cz_rs.at[k], d).wait_recv()

    for k in DIRECT:
        @pl.when(z + k < NZ)
        def _():
            clips_up(k).start()

    def spread(k, delta, half=None):
        ref, at = whole_or_half(slot(k, y), half), delta + NY * (half or 0)
        return remote(ref, ref, y_ss.at[k, at], y_rs.at[k, at], dev(z, lax.rem(y + delta, NY), c))

    def whole_or_half(at, half):
        if half is None:
            return far.at[at]
        return far.at[at, :, :, half * (HALF // 2) : (half + 1) * (HALF // 2)]

    def arrived(k, part):
        ref = far.at[slot(k, y), part]
        remote(ref, ref, z_ss.at[k, 0], z_rs.at[k, part], d).wait_recv()

    def arrived_whole(k):
        ref = far.at[slot(k, y)]
        remote(ref, ref, z_ss.at[k, 0], z_rs.at[k, 0], d).wait_recv()

    def forward():
        return remote(far.at[slot(2, y)], far.at[slot(3, y)], z_ss.at[3, 0], z_rs.at[3, 0], dev(z + 1, y, c))

    def leap():
        return remote(
            far.at[slot(2, y)], far.at[slot(4, y)], z_ss.at[4, 1], z_rs.at[4, 0], dev(jnp.minimum(z + 2, NZ - 1), y, c)
        )

    def backward():
        return remote(far.at[slot(5, y)], far.at[slot(4, y)], z_ss.at[4, 0], z_rs.at[4, 0], dev(z - 1, y, c))

    def spread_to(k):
        return (1, 3) if k in CHAINED else (2, 1, 3)

    def pass_on(k):
        @pl.when(z >= k)
        def _():
            if k in DIRECT:
                for part in range(NC):
                    arrived(k, part)
            else:
                arrived_whole(k)
            if k == 2:
                @pl.when(z < NZ - 1)
                def _():
                    forward().start()

                @pl.when((z >= LEAP) & (z <= NZ - 3))
                def _():
                    leap().start()
            if k == LEVELS + 1:
                @pl.when(z < LEAP + 3)
                def _():
                    backward().start()
            for delta in spread_to(k):
                if k <= LEVELS:
                    spread(k, delta, 0 if k in HALVED else None).start()
                else:
                    @pl.when(y + delta >= NY)
                    def _():
                        spread(k, delta).start()

    opposite = lax.rem(y + 2, NY)

    def chain(k):
        return remote(
            far.at[slot(k - 1, opposite)], far.at[slot(k, opposite)], x_ss.at[k], y_rs.at[k, 2], dev(z + 1, y, c)
        )

    def came(k, delta, half=None):
        ref, at = whole_or_half(slot(k, lax.rem(y + NY - delta, NY)), half), delta + NY * (half or 0)
        remote(ref, ref, y_ss.at[k, at], y_rs.at[k, at], d).wait_recv()

    def chain_on(k):
        if k not in CHAINED:
            return

        @pl.when(z >= k - 1)
        def _():
            came(k - 1, 2)

            @pl.when(z < NZ - 1)
            def _():
                chain(k).start()

    pass_on(1)

    wait_half(2)

    def cols(p):
        return pl.ds(pl.multiple_of(p * 128, 128), 128)

    def lanes(head, group):
        return slice(head * ROWS + group * 128, head * ROWS + (group + 1) * 128)

    first_rows = iota((128, 128), 0) < HEAD_DIM
    nothing = jnp.zeros((128, 128), jnp.bfloat16)
    for p in range(PAIRS):
        for group in range(2):
            part = qb[2 * group : 2 * group + 2, :, p * 128 : (p + 1) * 128].reshape(128, 128)
            turned = (part * jnp.bfloat16(HEAD_DIM ** -0.5)).T
            qm[p, :, lanes(0, group)] = jnp.where(first_rows, turned, nothing)
            qm[p, :, lanes(1, group)] = jnp.where(first_rows, nothing, turned)

    first_frame = iota((1, 128), 1) < TOK

    def own_frame(p, carry):
        def two_frames(ref, group):
            return ref[2 * group : 2 * group + 2, :, cols(p)].reshape(128, 128)

        keys = [two_frames(kb, group) for group in range(2)]
        values = [two_frames(vb, group) for group in range(2)]
        scores = []
        for head in range(2):
            for group in range(2):
                both = nn(keys[group], qm[p, :, lanes(head, group)])
                scores.append(jnp.where(first_frame, both[:TOK], both[TOK:]))
        scores = jnp.concatenate(scores, axis=1)
        top = jnp.max(scores, axis=0, keepdims=True)
        weights = jnp.exp(scores - top)
        tops[p] = top
        sums[p] = jnp.sum(weights, axis=0, keepdims=True)
        for head in range(2):
            for group in range(2):
                part = weights[:, lanes(head, group)]
                apart = jnp.concatenate(
                    [jnp.where(first_frame, part, 0.0), jnp.where(first_frame, 0.0, part)], axis=0
                ).astype(jnp.bfloat16)
                acc[p, :, lanes(head, group)] = tn(values[group], apart)[head * HEAD_DIM : (head + 1) * HEAD_DIM]
        return carry

    pass_on(2)
    pass_on(5)
    for k in (1, 2):
        @pl.when(z >= k)
        def _():
            clips_came(k)

    @pl.when((z >= 1) & (z < NZ - 2))
    def _():
        clips_on().start()

    lax.fori_loop(0, 3, own_frame, 0, unroll=3)
    chain_on(2)
    pass_on(3)
    pass_on(4)
    for k in HALVED:
        @pl.when(z >= k)
        def _():
            for delta in spread_to(k):
                spread(k, delta, 1).start()
    lax.fori_loop(3, PAIRS, own_frame, 0, unroll=3)

    for k in (3, LEVELS + 1):
        @pl.when(z >= k)
        def _():
            clips_came(k)
    table = clips[...].reshape(8, 128)
    own_first = BASE + 4 * y
    query_clip = [
        jnp.sum(jnp.where(lane == 4 * y + i, table[LEVELS + 1 : LEVELS + 2], 0.0), axis=1, keepdims=True)
        for i in range(FPC)
    ]
    table = table.astype(jnp.bfloat16)
    ones = jnp.ones((128, 128), jnp.bfloat16)

    def key_clips(numbers, rows):
        pick = (numbers // (NY * FPC))[:, :8] == iota((rows, 8), 1)
        level = jnp.dot(pick.astype(jnp.float32).astype(jnp.bfloat16), table, preferred_element_type=jnp.float32)
        one = jnp.where(lax.rem(numbers, NY * FPC) == iota((rows, 128), 1), level, 0.0)
        return jnp.dot(one.astype(jnp.bfloat16), ones, preferred_element_type=jnp.float32)

    def far_numbers(shape):
        n = iota(shape, 0)
        at, frame = n // BLK, lax.rem(n, BLK) // FAR
        step = at + NY - 1
        col = lax.rem(step, NY)
        level = functools.reduce(
            lambda found, k: jnp.where(step // NY == ORDER.index(k) + 1, k, found), ORDER, 0
        )
        regular = (LEVELS + 1 - level) * (NY * FPC) + col * FPC + frame
        shared = jnp.where(col < y, BASE, 0) + col * FPC + frame
        held = jnp.where((at >= MIXED) & (at < MIXED + NY), shared, regular)
        return jnp.where(at == OWN, own_first + frame, held)

    def near_numbers(shape):
        return own_first - 2 + iota(shape, 0) // NEAR_ROWS

    floor = (LEVELS + 1 - z) * (NY * FPC)
    for numbers, rows, bias in ((near_numbers, NKN, bias_near), (far_numbers, NKF, bias_far)):
        number = numbers((rows, 128))
        clip_of = key_clips(number, rows)
        for group in range(2):
            distance = own_first + 2 * group + lane // TOK - number
            seen = (distance >= 1) & (distance <= 2) if rows == NKN else distance > 2
            clip_here = jnp.where(first_frame, query_clip[2 * group], query_clip[2 * group + 1])
            ok = seen & (number >= floor) & (clip_of == clip_here)
            bias[:, group * 128 : (group + 1) * 128] = jnp.where(ok, 0.0, NEG)

    @pl.when(chip > 0)
    def _():
        for n in range(2):
            ref = near.at[n, pl.ds(0, 2 * NEAR_ROWS)]
            remote(ref, ref, near_ss.at[n], near_rs.at[n], d).wait_recv()

    chain_on(3)

    def level_here(k, half=None):
        @pl.when(z >= k)
        def _():
            for delta in range(1, NY):
                if not (delta == 2 and k + 1 in CHAINED):
                    came(k, delta, half)

    def shared_here():
        for delta in range(1, NY):
            @pl.when(y >= delta)
            def _():
                for part in range(NC):
                    ref = far.at[MIXED + lax.rem(y + NY - delta, NY), part]
                    remote(ref, ref, m_ss.at[delta, 0], m_rs.at[delta, part], d).wait_recv()

            @pl.when((y < delta) & (z >= LEVELS + 1))
            def _():
                came(LEVELS + 1, delta)

    ref = far.at[OWN, 1 - c]
    remote(ref, ref, own_ss.at[0], own_rs.at[0], d).wait_recv()

    theirs = pl.ds(2 * (1 - c), 2)

    def out_local(p):
        return pltpu.make_async_copy(
            ob.at[p, mine], out_hbm.at[:, :, pl.ds(pl.multiple_of(lo + p * 128, 128), 128)], o_ls.at[p]
        )

    def out_remote(p):
        return remote(
            ob.at[p, theirs], out_hbm.at[:, :, pl.ds(pl.multiple_of(lo + p * 128, 128), 128)],
            o_ss.at[p], o_rs.at[p], sibling,
        )

    def far_rows(p, first, last):
        rows = (last - first) * BLK
        both = far[first:last, :, :, cols(p)].astype(jnp.float32).reshape(rows // 8, 2, 8, 128)
        return [both[:, n].reshape(rows, 128).astype(jnp.bfloat16) for n in range(2)]

    def join(p, keys, values, bias):
        scores = nn(keys, qm[p]) + jnp.concatenate([bias, bias], axis=1)
        old = tops[p]
        top = jnp.maximum(old, jnp.max(scores, axis=0, keepdims=True))
        factor = jnp.exp(old - top)
        weights = jnp.exp(scores - top)
        total = sums[p] * factor + jnp.sum(weights, axis=0, keepdims=True)
        weights = weights.astype(jnp.bfloat16)
        turned = values.T
        summed = [
            nn(turned[n * HEAD_DIM : (n + 1) * HEAD_DIM], weights[:, n * ROWS : (n + 1) * ROWS]) for n in range(2)
        ]
        return top, total, acc[p] * factor + jnp.concatenate(summed, axis=1)

    def keep(part):
        joined = [join(p, *part(p)) for p in range(PAIRS)]
        for p, (top, total, summed) in enumerate(joined):
            tops[p], sums[p], acc[p] = top, total, summed

    def nearest(p):
        keys, values = far_rows(p, 0, CHUNKS[0])
        keys = jnp.concatenate([near[0, :NKN, cols(p)], keys], axis=0)
        values = jnp.concatenate([near[1, :NKN, cols(p)], values], axis=0)
        return keys, values, jnp.concatenate([bias_near[...], bias_far[: CHUNKS[0] * BLK]], axis=0)

    def middle(p):
        return *far_rows(p, *CHUNKS), bias_far[CHUNKS[0] * BLK : CHUNKS[1] * BLK]

    def put(p, total, summed):
        result = (summed / total).astype(jnp.bfloat16)
        for group in range(2):
            turned = jnp.concatenate([result[:, lanes(head, group)] for head in range(2)], axis=0).T
            ob[p, 2 * group] = turned[:TOK]
            ob[p, 2 * group + 1] = turned[TOK:]

    level_here(1)
    keep(nearest)
    level_here(2)
    shared_here()
    keep(middle)
    def send_out(group):
        for p in group:
            out_remote(p).start()
            out_local(p).start()

    groups = (range(0, 3), range(3, PAIRS))

    @pl.when(z >= 3)
    def _():
        for half, group in enumerate(groups):
            for k in HALVED:
                level_here(k, half)
            for p in group:
                put(p, *join(p, *far_rows(p, CHUNKS[1], SLOTS), bias_far[CHUNKS[1] * BLK :])[1:])
            send_out(group)

    @pl.when(z < 3)
    def _():
        for group in groups:
            for p in group:
                put(p, sums[p], acc[p])
            send_out(group)

    for p in range(PAIRS):
        out_local(p).wait()
        out_remote(p).wait_send()
        ref = out_hbm.at[:, :, pl.ds(pl.multiple_of(hi + p * 128, 128), 128)]
        remote(ref, ref, o_ss.at[p], o_rs.at[p], sibling).wait_recv()
    for n in range(3):
        halves[n].wait_send()
    for cp in level_sends:
        cp.wait_send()
    across.wait_send()
    each_rise(lambda cp: cp.wait_send())
    each_mixed(lambda cp: cp.wait_send())

    @pl.when((z >= LEVELS + 1) & (z < LEAP + 3))
    def _():
        backward().wait_send()

    @pl.when((z >= 2) & (z < NZ - 1))
    def _():
        forward().wait_send()

    for k in CHAINED:
        @pl.when((z >= k - 1) & (z < NZ - 1))
        def _():
            chain(k).wait_send()

    for k in DIRECT:
        @pl.when(z + k < NZ)
        def _():
            clips_up(k).wait_send()

    @pl.when((z >= 1) & (z < NZ - 2))
    def _():
        clips_on().wait_send()

    @pl.when((z >= LEAP) & (z <= NZ - 3))
    def _():
        leap().wait_send()

    @pl.when(chip < NZ * NY - 1)
    def _():
        for n in range(2):
            near_out(n).wait_send()

    for k in ORDER:
        for delta in spread_to(k):
            @pl.when((z >= k) if k <= LEVELS else ((z >= k) & (y + delta >= NY)))
            def _():
                for half in (0, 1) if k in HALVED else (None,):
                    spread(k, delta, half).wait_send()


def on_device(queries, key_states, value_states, clip_ids):
    bf, f32 = jnp.bfloat16, jnp.float32
    dma = pltpu.SemaphoreType.DMA
    anywhere = pl.BlockSpec(memory_space=pltpu.HBM)
    return pl.pallas_call(
        kernel,
        out_shape=jax.ShapeDtypeStruct(queries.shape, bf),
        in_specs=[anywhere] * 4,
        out_specs=anywhere,
        scratch_shapes=[
            pltpu.SMEM((2,), jnp.int32),
            pltpu.VMEM((2, TOK, 2 * HALF), bf),
            pltpu.VMEM((2, TOK, 2 * HALF), bf),
            pltpu.VMEM((FPC, TOK, HALF), bf),
            pltpu.VMEM((FPC, TOK, HALF), bf),
            pltpu.VMEM((FPC, TOK, HALF), bf),
            pltpu.VMEM((2, BLK, HALF), bf),
            pltpu.VMEM((SLOTS, NC, BLK, HALF), bf),
            pltpu.VMEM((2, 6 * NEAR_ROWS, HALF), bf),
            pltpu.VMEM((PAIRS, 128, LANES), bf),
            pltpu.VMEM((NY * NC, 1, 128), f32),
            pltpu.VMEM((8, 1, 128), f32),
            pltpu.VMEM((NKF, ROWS), f32),
            pltpu.VMEM((NKN, ROWS), f32),
            pltpu.VMEM((PAIRS, HEAD_DIM, LANES), f32),
            pltpu.VMEM((PAIRS, 1, LANES), f32),
            pltpu.VMEM((PAIRS, 1, LANES), f32),
            pltpu.VMEM((PAIRS, FPC, TOK, 128), bf),
            dma((6,)),
            dma((3,)), dma((3,)),
            dma((1,)), dma((1,)),
            dma((LEVELS + 2, NC)), dma((LEVELS + 2, NC)),
            dma((NY, NC)), dma((NY, NC)),
            dma((LEVELS + 2, 2 * NY)), dma((LEVELS + 2, 2 * NY)), dma((LEVELS + 2,)),
            dma((2,)), dma((2,)),
            dma((NY * NC,)), dma((NY * NC,)),
            dma((LEVELS + 2,)), dma((LEVELS + 2,)),
            dma((PAIRS,)), dma((PAIRS,)), dma((PAIRS,)),
        ],
        compiler_params=pltpu.CompilerParams(
            collective_id=0, has_side_effects=True, vmem_limit_bytes=64 << 20
        ),
        cost_estimate=pl.CostEstimate(flops=1 << 30, bytes_accessed=4 << 20, transcendentals=1 << 21),
    )(queries, key_states, value_states, clip_ids)


def solution(mesh):
    frames = P(("dp", "tm"), None, None)
    return jax.shard_map(
        on_device,
        mesh=mesh,
        in_specs=(frames, frames, frames, P(("dp", "tm"))),
        out_specs=frames,
        check_vma=False,
    )
```

```python
import functools

import jax
import jax.numpy as jnp
from jax import lax
from jax.experimental import pallas as pl
from jax.experimental.pallas import tpu as pltpu
from jax.sharding import PartitionSpec as P

HEAD_DIM = 64
SIDE = 8
TOK = 64
NZ, NY, NC = 8, 4, 2
FPC = 4
HALF = 768
PAIRS = HALF // 128
ROWS = FPC * TOK
LANES = 2 * ROWS
FAR = 4
BLK = FPC * FAR
LEVELS = 4
OWN = 0
ORDER = (1, 2, 5, 3, 4)
FIRST = {k: 1 + n * NY for n, k in enumerate(ORDER)}
DIRECT = (1, 2, 5)
LEAP = 3
HALVED = (3, 4)
CHAINED = (2,)
MIXED = FIRST[LEVELS + 1]
SLOTS = 1 + 5 * NY
CHUNKS = (FIRST[2], FIRST[3])
NKF = SLOTS * BLK
NEAR_ROWS = 16
NKN = 5 * NEAR_ROWS
FLAT = (LEVELS + 2) * NY * FPC
BASE = FLAT - NY * FPC
NEG = -1e30
MESH = pl.DeviceIdType.MESH


def iota(shape, dim):
    return lax.broadcasted_iota(jnp.int32, shape, dim)


def remote(src, dst, ss, rs, to):
    return pltpu.make_async_remote_copy(
        src_ref=src, dst_ref=dst, send_sem=ss, recv_sem=rs, device_id={"tm": to}, device_id_type=MESH
    )


def nt(a, b):
    return lax.dot_general(a, b, (((1,), (1,)), ((), ())), preferred_element_type=jnp.float32)


def nn(a, b):
    return jnp.dot(a, b, preferred_element_type=jnp.float32)


def tn(a, b):
    return lax.dot_general(a, b, (((0,), (0,)), ((), ())), preferred_element_type=jnp.float32)


def kernel(
    q_hbm, k_hbm, v_hbm, clip_hbm, out_hbm,
    clip_ref, kf, vf, qb, kb, vb, pooled, far, near, qm, level_clips, clips, bias_far, bias_near, acc, tops, sums, ob,
    in_sem, sib_ss, sib_rs, own_ss, own_rs, z_ss, z_rs, m_ss, m_rs, y_ss, y_rs, x_ss,
    near_ss, near_rs, cy_ss, cy_rs, cz_ss, cz_rs, o_ss, o_rs, o_ls,
):
    d = lax.axis_index("tm")
    z, y, c = d // (NY * NC), lax.rem(d // NC, NY), lax.rem(d, NC)
    chip = d // NC

    def dev(zz, yy, cc):
        return zz * (NY * NC) + yy * NC + cc

    sibling = dev(z, y, 1 - c)

    barrier = pltpu.get_barrier_semaphore()

    def greet(to):
        pl.semaphore_signal(barrier, inc=1, device_id={"tm": to}, device_id_type=MESH)

    for k in DIRECT[::-1]:
        @pl.when(z >= k)
        def _():
            for core in range(NC):
                greet(dev(z - k, y, core))

    @pl.when((y == 0) & (z > 0))
    def _():
        greet(dev(z - 1, NY - 1, c))

    for yy in range(1, NY):
        for cc in range(NC):
            greet(dev(z, lax.rem(y + yy, NY), cc))
    greet(sibling)

    lo = pl.multiple_of(c * HALF, 128)
    hi = pl.multiple_of((1 - c) * HALF, 128)
    mine = pl.ds(2 * c, 2)
    whole = []
    for n, (src, dst) in enumerate(((k_hbm, kf), (v_hbm, vf))):
        cp = pltpu.make_async_copy(src, dst, in_sem.at[n])
        cp.start()
        whole.append(cp)
    clip_copy = pltpu.make_async_copy(clip_hbm, clip_ref, in_sem.at[2])
    clip_copy.start()
    local = []
    for n, (src, dst) in enumerate(((k_hbm, kb), (v_hbm, vb), (q_hbm, qb))):
        cp = pltpu.make_async_copy(src.at[:, :, pl.ds(lo, HALF)], dst.at[mine], in_sem.at[3 + n])
        cp.start()
        local.append(cp)

    for k in ORDER:
        for col in range(NY):
            @pl.when((z < k) & (col >= y) if k == LEVELS + 1 else z < k)
            def _():
                far[FIRST[k] + col] = jnp.zeros(far.shape[1:], far.dtype)

    @pl.when(chip == 0)
    def _():
        near[:, : 2 * NEAR_ROWS] = jnp.zeros((2, 2 * NEAR_ROWS, HALF), jnp.bfloat16)

    for k in range(1, LEVELS + 2):
        @pl.when(z < (3 if k == LEVELS else k))
        def _():
            clips[LEVELS + 1 - k] = jnp.zeros((1, 128), jnp.float32)
    for n in range(LEVELS + 2, 8):
        clips[n] = jnp.zeros((1, 128), jnp.float32)

    def pool_matrix(rows, frames, side):
        r, t = iota((rows, frames * TOK), 0), iota((rows, frames * TOK), 1)
        frame, token = t // TOK, lax.rem(t, TOK)
        cells = SIDE // side
        at = frame * cells * cells + (token // SIDE // side) * cells + lax.rem(token, SIDE) // side
        return jnp.where(r == at, 1.0 / (side * side), 0.0).astype(jnp.bfloat16)

    far_pool = pool_matrix(2 * FAR, 2, 4)
    means = []
    for n, full in enumerate((kf, vf)):
        whole[n].wait()
        means.append(nn(far_pool, full[...].reshape(2 * TOK, 2 * HALF)))
    means = jnp.concatenate(means, axis=0).astype(jnp.bfloat16)
    for n in range(2):
        pooled[n] = means[:, n * HALF : (n + 1) * HALF]

    up = sum(jnp.where(z + k < NZ, NC, 0) for k in DIRECT)
    next_near = jnp.where((y == NY - 1) & (z < NZ - 1), 1, 0)
    pl.semaphore_wait(barrier, (NY - 1) * NC + 1 + up + next_near)

    def slot(k, col):
        return FIRST[k] + col

    def rise(k, core):
        return remote(
            pooled.at[core], far.at[slot(k, y), c], z_ss.at[k, core], z_rs.at[k, c], dev(z + k, y, core)
        )

    def mixed(delta, core):
        return remote(
            pooled.at[core], far.at[MIXED + y, c], m_ss.at[delta, core], m_rs.at[delta, c],
            dev(z, lax.rem(y + delta, NY), core),
        )

    def each_rise(act):
        for k in (5, 1, 2):
            @pl.when(z + k < NZ)
            def _():
                for core in range(NC):
                    act(rise(k, core))

    def each_mixed(act):
        for delta in (1, 3, 2):
            @pl.when(y + delta < NY)
            def _():
                for core in range(NC):
                    act(mixed(delta, core))

    each_rise(lambda cp: cp.start())
    each_mixed(lambda cp: cp.start())
    across = remote(pooled.at[1 - c], far.at[OWN, c], own_ss.at[0], own_rs.at[0], sibling)
    across.start()
    far[OWN, c] = pooled[c]

    halves = []
    for n, (src, dst) in enumerate(((k_hbm, kb), (v_hbm, vb), (q_hbm, qb))):
        cp = remote(src.at[:, :, pl.ds(hi, HALF)], dst.at[mine], sib_ss.at[n], sib_rs.at[n], sibling)
        cp.start()
        halves.append(cp)

    def wait_half(n):
        local[n].wait()
        other = (kb, vb, qb)[n].at[pl.ds(2 * (1 - c), 2)]
        remote(other, other, sib_ss.at[n], sib_rs.at[n], sibling).wait_recv()

    clip_copy.wait()
    row = y * NC + c
    lane = iota((1, 128), 1)
    level_clips[row] = sum(
        jnp.where(lane == 2 * row + n, clip_ref[n].astype(jnp.float32), 0.0) for n in range(2)
    )
    level_sends = []
    for n in range(1, NY * NC):
        to = lax.rem(row + n, NY * NC)
        ref = level_clips.at[row]
        cp = remote(ref, ref, cy_ss.at[n], cy_rs.at[n], z * (NY * NC) + to)
        cp.start()
        level_sends.append(cp)

    near_pool = pool_matrix(NEAR_ROWS * FPC, FPC, 2)
    for n, full in enumerate((kb, vb)):
        wait_half(n)
        near[n, 2 * NEAR_ROWS :] = nn(near_pool, full[...].reshape(ROWS, HALF)).astype(jnp.bfloat16)

    near_out = remote(
        near.at[:, pl.ds(4 * NEAR_ROWS, 2 * NEAR_ROWS)], near.at[:, pl.ds(0, 2 * NEAR_ROWS)],
        near_ss.at[0], near_rs.at[0], jnp.minimum((chip + 1) * NC + c, NZ * NY * NC - 1),
    )

    @pl.when(chip < NZ * NY - 1)
    def _():
        near_out.start()

    for n in range(1, NY * NC):
        ref = level_clips.at[lax.rem(row + NY * NC - n, NY * NC)]
        remote(ref, ref, cy_ss.at[n], cy_rs.at[n], d).wait_recv()
    clips[LEVELS + 1] = jnp.sum(level_clips[...], axis=0)
    def clips_up(k):
        return remote(
            clips.at[LEVELS + 1], clips.at[LEVELS + 1 - k], cz_ss.at[k], cz_rs.at[k], dev(z + k, y, c)
        )

    def clips_on():
        return remote(clips.at[3:5], clips.at[1:3], cz_ss.at[3], cz_rs.at[3], dev(z + 2, y, c))

    def clips_came(k):
        ref = clips.at[1:3] if k == 3 else clips.at[LEVELS + 1 - k]
        remote(ref, ref, cz_ss.at[k], cz_rs.at[k], d).wait_recv()

    for k in DIRECT:
        @pl.when(z + k < NZ)
        def _():
            clips_up(k).start()

    def spread(k, delta, half=None):
        ref, at = whole_or_half(slot(k, y), half), delta + NY * (half or 0)
        return remote(ref, ref, y_ss.at[k, at], y_rs.at[k, at], dev(z, lax.rem(y + delta, NY), c))

    def whole_or_half(at, half):
        if half is None:
            return far.at[at]
        return far.at[at, :, :, half * (HALF // 2) : (half + 1) * (HALF // 2)]

    def arrived(k, part):
        ref = far.at[slot(k, y), part]
        remote(ref, ref, z_ss.at[k, 0], z_rs.at[k, part], d).wait_recv()

    def arrived_whole(k):
        ref = far.at[slot(k, y)]
        remote(ref, ref, z_ss.at[k, 0], z_rs.at[k, 0], d).wait_recv()

    def forward():
        return remote(far.at[slot(2, y)], far.at[slot(3, y)], z_ss.at[3, 0], z_rs.at[3, 0], dev(z + 1, y, c))

    def leap():
        return remote(
            far.at[slot(2, y)], far.at[slot(4, y)], z_ss.at[4, 1], z_rs.at[4, 0], dev(jnp.minimum(z + 2, NZ - 1), y, c)
        )

    def backward():
        return remote(far.at[slot(5, y)], far.at[slot(4, y)], z_ss.at[4, 0], z_rs.at[4, 0], dev(z - 1, y, c))

    def spread_to(k):
        return (1, 3) if k in CHAINED else (2, 1, 3)

    def pass_on(k):
        @pl.when(z >= k)
        def _():
            if k in DIRECT:
                for part in range(NC):
                    arrived(k, part)
            else:
                arrived_whole(k)
            if k == 2:
                @pl.when(z < NZ - 1)
                def _():
                    forward().start()

                @pl.when((z >= LEAP) & (z <= NZ - 3))
                def _():
                    leap().start()
            if k == LEVELS + 1:
                @pl.when(z < LEAP + 3)
                def _():
                    backward().start()
            for delta in spread_to(k):
                if k <= LEVELS:
                    spread(k, delta, 0 if k in HALVED else None).start()
                else:
                    @pl.when(y + delta >= NY)
                    def _():
                        spread(k, delta).start()

    opposite = lax.rem(y + 2, NY)

    def chain(k):
        return remote(
            far.at[slot(k - 1, opposite)], far.at[slot(k, opposite)], x_ss.at[k], y_rs.at[k, 2], dev(z + 1, y, c)
        )

    def came(k, delta, half=None):
        ref, at = whole_or_half(slot(k, lax.rem(y + NY - delta, NY)), half), delta + NY * (half or 0)
        remote(ref, ref, y_ss.at[k, at], y_rs.at[k, at], d).wait_recv()

    def chain_on(k):
        if k not in CHAINED:
            return

        @pl.when(z >= k - 1)
        def _():
            came(k - 1, 2)

            @pl.when(z < NZ - 1)
            def _():
                chain(k).start()

    pass_on(1)

    wait_half(2)

    def cols(p):
        return pl.ds(pl.multiple_of(p * 128, 128), 128)

    def lanes(head, group):
        return slice(head * ROWS + group * 128, head * ROWS + (group + 1) * 128)

    first_rows = iota((128, 128), 0) < HEAD_DIM
    nothing = jnp.zeros((128, 128), jnp.bfloat16)
    for p in range(PAIRS):
        for group in range(2):
            part = qb[2 * group : 2 * group + 2, :, p * 128 : (p + 1) * 128].reshape(128, 128)
            turned = (part * jnp.bfloat16(HEAD_DIM ** -0.5)).T
            qm[p, :, lanes(0, group)] = jnp.where(first_rows, turned, nothing)
            qm[p, :, lanes(1, group)] = jnp.where(first_rows, nothing, turned)

    first_frame = iota((1, 128), 1) < TOK

    def own_frame(p, carry):
        def two_frames(ref, group):
            return ref[2 * group : 2 * group + 2, :, cols(p)].reshape(128, 128)

        keys = [two_frames(kb, group) for group in range(2)]
        values = [two_frames(vb, group) for group in range(2)]
        scores = []
        for head in range(2):
            for group in range(2):
                both = nn(keys[group], qm[p, :, lanes(head, group)])
                scores.append(jnp.where(first_frame, both[:TOK], both[TOK:]))
        scores = jnp.concatenate(scores, axis=1)
        top = jnp.max(scores, axis=0, keepdims=True)
        weights = jnp.exp(scores - top)
        tops[p] = top
        sums[p] = jnp.sum(weights, axis=0, keepdims=True)
        for head in range(2):
            for group in range(2):
                part = weights[:, lanes(head, group)]
                apart = jnp.concatenate(
                    [jnp.where(first_frame, part, 0.0), jnp.where(first_frame, 0.0, part)], axis=0
                ).astype(jnp.bfloat16)
                acc[p, :, lanes(head, group)] = tn(values[group], apart)[head * HEAD_DIM : (head + 1) * HEAD_DIM]
        return carry

    pass_on(2)
    pass_on(5)
    for k in (1, 2):
        @pl.when(z >= k)
        def _():
            clips_came(k)

    @pl.when((z >= 1) & (z < NZ - 2))
    def _():
        clips_on().start()

    lax.fori_loop(0, 3, own_frame, 0, unroll=3)
    chain_on(2)
    pass_on(3)
    pass_on(4)
    for k in HALVED:
        @pl.when(z >= k)
        def _():
            for delta in spread_to(k):
                spread(k, delta, 1).start()
    lax.fori_loop(3, PAIRS, own_frame, 0, unroll=3)

    for k in (3, LEVELS + 1):
        @pl.when(z >= k)
        def _():
            clips_came(k)
    table = clips[...].reshape(8, 128)
    own_first = BASE + 4 * y
    query_clip = [
        jnp.sum(jnp.where(lane == 4 * y + i, table[LEVELS + 1 : LEVELS + 2], 0.0), axis=1, keepdims=True)
        for i in range(FPC)
    ]
    table = table.astype(jnp.bfloat16)
    ones = jnp.ones((128, 128), jnp.bfloat16)

    def key_clips(numbers, rows):
        pick = (numbers // (NY * FPC))[:, :8] == iota((rows, 8), 1)
        level = jnp.dot(pick.astype(jnp.float32).astype(jnp.bfloat16), table, preferred_element_type=jnp.float32)
        one = jnp.where(lax.rem(numbers, NY * FPC) == iota((rows, 128), 1), level, 0.0)
        return jnp.dot(one.astype(jnp.bfloat16), ones, preferred_element_type=jnp.float32)

    def far_numbers(shape):
        n = iota(shape, 0)
        at, frame = n // BLK, lax.rem(n, BLK) // FAR
        step = at + NY - 1
        col = lax.rem(step, NY)
        level = functools.reduce(
            lambda found, k: jnp.where(step // NY == ORDER.index(k) + 1, k, found), ORDER, 0
        )
        regular = (LEVELS + 1 - level) * (NY * FPC) + col * FPC + frame
        shared = jnp.where(col < y, BASE, 0) + col * FPC + frame
        held = jnp.where((at >= MIXED) & (at < MIXED + NY), shared, regular)
        return jnp.where(at == OWN, own_first + frame, held)

    def near_numbers(shape):
        return own_first - 2 + iota(shape, 0) // NEAR_ROWS

    floor = (LEVELS + 1 - z) * (NY * FPC)
    for numbers, rows, bias in ((near_numbers, NKN, bias_near), (far_numbers, NKF, bias_far)):
        number = numbers((rows, 128))
        clip_of = key_clips(number, rows)
        for group in range(2):
            distance = own_first + 2 * group + lane // TOK - number
            seen = (distance >= 1) & (distance <= 2) if rows == NKN else distance > 2
            clip_here = jnp.where(first_frame, query_clip[2 * group], query_clip[2 * group + 1])
            ok = seen & (number >= floor) & (clip_of == clip_here)
            bias[:, group * 128 : (group + 1) * 128] = jnp.where(ok, 0.0, NEG)

    @pl.when(chip > 0)
    def _():
        ref = near.at[:, pl.ds(0, 2 * NEAR_ROWS)]
        remote(ref, ref, near_ss.at[0], near_rs.at[0], d).wait_recv()

    chain_on(3)

    def level_here(k, half=None):
        @pl.when(z >= k)
        def _():
            for delta in range(1, NY):
                if not (delta == 2 and k + 1 in CHAINED):
                    came(k, delta, half)

    def shared_here():
        for delta in range(1, NY):
            @pl.when(y >= delta)
            def _():
                for part in range(NC):
                    ref = far.at[MIXED + lax.rem(y + NY - delta, NY), part]
                    remote(ref, ref, m_ss.at[delta, 0], m_rs.at[delta, part], d).wait_recv()

            @pl.when((y < delta) & (z >= LEVELS + 1))
            def _():
                came(LEVELS + 1, delta)

    ref = far.at[OWN, 1 - c]
    remote(ref, ref, own_ss.at[0], own_rs.at[0], d).wait_recv()

    theirs = pl.ds(2 * (1 - c), 2)

    def out_local(p):
        return pltpu.make_async_copy(
            ob.at[p, mine], out_hbm.at[:, :, pl.ds(pl.multiple_of(lo + p * 128, 128), 128)], o_ls.at[p]
        )

    def out_remote(p):
        return remote(
            ob.at[p, theirs], out_hbm.at[:, :, pl.ds(pl.multiple_of(lo + p * 128, 128), 128)],
            o_ss.at[p], o_rs.at[p], sibling,
        )

    def far_rows(p, first, last):
        rows = (last - first) * BLK
        both = far[first:last, :, :, cols(p)].astype(jnp.float32).reshape(rows // 8, 2, 8, 128)
        return [both[:, n].reshape(rows, 128).astype(jnp.bfloat16) for n in range(2)]

    def join(p, keys, values, bias):
        scores = nn(keys, qm[p]) + jnp.concatenate([bias, bias], axis=1)
        old = tops[p]
        top = jnp.maximum(old, jnp.max(scores, axis=0, keepdims=True))
        factor = jnp.exp(old - top)
        weights = jnp.exp(scores - top)
        total = sums[p] * factor + jnp.sum(weights, axis=0, keepdims=True)
        weights = weights.astype(jnp.bfloat16)
        turned = values.T
        summed = [
            nn(turned[n * HEAD_DIM : (n + 1) * HEAD_DIM], weights[:, n * ROWS : (n + 1) * ROWS]) for n in range(2)
        ]
        return top, total, acc[p] * factor + jnp.concatenate(summed, axis=1)

    def keep(part):
        joined = [join(p, *part(p)) for p in range(PAIRS)]
        for p, (top, total, summed) in enumerate(joined):
            tops[p], sums[p], acc[p] = top, total, summed

    def nearest(p):
        keys, values = far_rows(p, 0, CHUNKS[0])
        keys = jnp.concatenate([near[0, :NKN, cols(p)], keys], axis=0)
        values = jnp.concatenate([near[1, :NKN, cols(p)], values], axis=0)
        return keys, values, jnp.concatenate([bias_near[...], bias_far[: CHUNKS[0] * BLK]], axis=0)

    def middle(p):
        return *far_rows(p, *CHUNKS), bias_far[CHUNKS[0] * BLK : CHUNKS[1] * BLK]

    def put(p, total, summed):
        result = (summed / total).astype(jnp.bfloat16)
        for group in range(2):
            turned = jnp.concatenate([result[:, lanes(head, group)] for head in range(2)], axis=0).T
            ob[p, 2 * group] = turned[:TOK]
            ob[p, 2 * group + 1] = turned[TOK:]

    level_here(1)
    keep(nearest)
    level_here(2)
    shared_here()
    keep(middle)
    def send_out(group):
        for p in group:
            out_remote(p).start()
            out_local(p).start()

    groups = (range(0, 3), range(3, PAIRS))

    @pl.when(z >= 3)
    def _():
        for half, group in enumerate(groups):
            for k in HALVED:
                level_here(k, half)
            for p in group:
                put(p, *join(p, *far_rows(p, CHUNKS[1], SLOTS), bias_far[CHUNKS[1] * BLK :])[1:])
            send_out(group)

    @pl.when(z < 3)
    def _():
        for group in groups:
            for p in group:
                put(p, sums[p], acc[p])
            send_out(group)

    for p in range(PAIRS):
        out_local(p).wait()
        out_remote(p).wait_send()
        ref = out_hbm.at[:, :, pl.ds(pl.multiple_of(hi + p * 128, 128), 128)]
        remote(ref, ref, o_ss.at[p], o_rs.at[p], sibling).wait_recv()
    for n in range(3):
        halves[n].wait_send()
    for cp in level_sends:
        cp.wait_send()
    across.wait_send()
    each_rise(lambda cp: cp.wait_send())
    each_mixed(lambda cp: cp.wait_send())

    @pl.when((z >= LEVELS + 1) & (z < LEAP + 3))
    def _():
        backward().wait_send()

    @pl.when((z >= 2) & (z < NZ - 1))
    def _():
        forward().wait_send()

    for k in CHAINED:
        @pl.when((z >= k - 1) & (z < NZ - 1))
        def _():
            chain(k).wait_send()

    for k in DIRECT:
        @pl.when(z + k < NZ)
        def _():
            clips_up(k).wait_send()

    @pl.when((z >= 1) & (z < NZ - 2))
    def _():
        clips_on().wait_send()

    @pl.when((z >= LEAP) & (z <= NZ - 3))
    def _():
        leap().wait_send()

    @pl.when(chip < NZ * NY - 1)
    def _():
        near_out.wait_send()

    for k in ORDER:
        for delta in spread_to(k):
            @pl.when((z >= k) if k <= LEVELS else ((z >= k) & (y + delta >= NY)))
            def _():
                for half in (0, 1) if k in HALVED else (None,):
                    spread(k, delta, half).wait_send()


def on_device(queries, key_states, value_states, clip_ids):
    bf, f32 = jnp.bfloat16, jnp.float32
    dma = pltpu.SemaphoreType.DMA
    anywhere = pl.BlockSpec(memory_space=pltpu.HBM)
    return pl.pallas_call(
        kernel,
        out_shape=jax.ShapeDtypeStruct(queries.shape, bf),
        in_specs=[anywhere] * 4,
        out_specs=anywhere,
        scratch_shapes=[
            pltpu.SMEM((2,), jnp.int32),
            pltpu.VMEM((2, TOK, 2 * HALF), bf),
            pltpu.VMEM((2, TOK, 2 * HALF), bf),
            pltpu.VMEM((FPC, TOK, HALF), bf),
            pltpu.VMEM((FPC, TOK, HALF), bf),
            pltpu.VMEM((FPC, TOK, HALF), bf),
            pltpu.VMEM((2, BLK, HALF), bf),
            pltpu.VMEM((SLOTS, NC, BLK, HALF), bf),
            pltpu.VMEM((2, 6 * NEAR_ROWS, HALF), bf),
            pltpu.VMEM((PAIRS, 128, LANES), bf),
            pltpu.VMEM((NY * NC, 1, 128), f32),
            pltpu.VMEM((8, 1, 128), f32),
            pltpu.VMEM((NKF, ROWS), f32),
            pltpu.VMEM((NKN, ROWS), f32),
            pltpu.VMEM((PAIRS, HEAD_DIM, LANES), f32),
            pltpu.VMEM((PAIRS, 1, LANES), f32),
            pltpu.VMEM((PAIRS, 1, LANES), f32),
            pltpu.VMEM((PAIRS, FPC, TOK, 128), bf),
            dma((6,)),
            dma((3,)), dma((3,)),
            dma((1,)), dma((1,)),
            dma((LEVELS + 2, NC)), dma((LEVELS + 2, NC)),
            dma((NY, NC)), dma((NY, NC)),
            dma((LEVELS + 2, 2 * NY)), dma((LEVELS + 2, 2 * NY)), dma((LEVELS + 2,)),
            dma((1,)), dma((1,)),
            dma((NY * NC,)), dma((NY * NC,)),
            dma((LEVELS + 2,)), dma((LEVELS + 2,)),
            dma((PAIRS,)), dma((PAIRS,)), dma((PAIRS,)),
        ],
        compiler_params=pltpu.CompilerParams(
            collective_id=0, has_side_effects=True, vmem_limit_bytes=64 << 20
        ),
        cost_estimate=pl.CostEstimate(flops=1 << 30, bytes_accessed=4 << 20, transcendentals=1 << 21),
    )(queries, key_states, value_states, clip_ids)


def solution(mesh):
    frames = P(("dp", "tm"), None, None)
    return jax.shard_map(
        on_device,
        mesh=mesh,
        in_specs=(frames, frames, frames, P(("dp", "tm"))),
        out_specs=frames,
        check_vma=False,
    )
```
